128 devices in a mesh: dp: 2 (over x_lo), tm: 16 (over z, y), head: 4 (over x_hi, core).
Axes of the slice: x: 4 (x_hi: 2, x_lo: 2; x = x_hi * 2 + x_lo), y: 4, z: 4, core: 2. Of those that a mesh axis runs over, the one named last changes fastest.
Arguments:
- clip: bfloat16 [32, 1792, 1152], P(('dp', 'tm'), 'head'), parts along dimension 0, may hold values from -8 to 8
- modulation: float32 [12, 1152], P('dp'), parts along dimension 0, may hold values from -3 to 3
- w_qkv_s: bfloat16 [1152, 3456], replicated, may hold values from -1.9 to 1.9
- w_out_s: bfloat16 [1152, 1152], replicated, may hold values from -0.1875 to 0.1875
- w_qkv_t: bfloat16 [1152, 3456], replicated, may hold values from -1.9 to 1.9
- w_out_t: bfloat16 [1152, 1152], replicated, may hold values from -0.1875 to 0.1875
Outputs:
- result: bfloat16 [32, 1792, 1152], P(('dp', 'tm'), 'head'), parts along dimension 0
The draws below stay inside these ranges and needn't reach their ends.
There are 2 independent parts, one for each index of `dp`. The reference program is written for one: setup_inputs(seed, part) draws one part's arguments, and reference() takes and returns one part's arrays. A program takes and returns all parts, laid end to end along the dimension named above; an argument that names none is the same for every part. Nothing has to cross between parts.
All inputs are finite; a program needn't handle non-finite values.
Results may differ from the reference program's by a relative error of at most 0.017.
Values may be sent and summed in bfloat16 or wider, within the bound.
No kernel may reach another device: no remote copies, remote signals or barrier semaphores. Data moves between devices by JAX's collectives and lax.ppermute only.
A program may use at most 192 MiB of HBM per device.

```python
import math
import jax
import jax.numpy as jnp
from jax import lax

D = 1152
HEADS = 16
HEAD_DIM = 72
F = 16
S = 1792


def draw_clip(key, part):
    key = jax.random.fold_in(key, 11)
    first = jax.random.fold_in(key, 0)
    base = jnp.clip(jax.random.normal(first, (F, S, D), jnp.float32), -8.0, 8.0)
    return base.astype(jnp.bfloat16)


def projection_weight(key):
    first, second, third = jax.random.split(key, 3)
    spread = D ** (-0.5)
    query_part = spread * jax.random.normal(first, (D, D), jnp.float32)
    key_part = spread * jax.random.normal(second, (D, D), jnp.float32)
    value_part = spread * jax.random.normal(third, (D, D), jnp.float32)
    joined = jnp.concatenate([query_part, key_part, value_part], axis=1)
    return jnp.clip(joined, -1.9, 1.9).astype(jnp.bfloat16)


def draw_w_qkv_s(key, part):
    key = jax.random.fold_in(key, 21)
    return projection_weight(key)


def draw_w_qkv_t(key, part):
    key = jax.random.fold_in(key, 22)
    return projection_weight(key)


def gaussian(own_key, extent, scale, most, dtype=jnp.bfloat16):
    return jnp.clip(scale * jax.random.normal(own_key, extent, jnp.float32), -most, most).astype(dtype)


def setup_inputs(seed: int = 0, part: int = 0) -> dict:
    arg_keys = jax.random.split(jax.random.key(seed), 7)
    part_keys = jax.random.split(jax.random.fold_in(arg_keys[6], part), 7)
    return {
        "clip": draw_clip(jax.random.fold_in(jax.random.fold_in(arg_keys[6], part), 71), part),
        "modulation": gaussian(part_keys[1], (6, D), 0.5, 3.0, jnp.float32),
        "w_qkv_s": draw_w_qkv_s(jax.random.fold_in(arg_keys[6], 71), part),
        "w_out_s": gaussian(arg_keys[3], (D, D), D ** -0.5, 0.1875),
        "w_qkv_t": draw_w_qkv_t(jax.random.fold_in(arg_keys[6], 71), part),
        "w_out_t": gaussian(arg_keys[5], (D, D), D ** -0.5, 0.1875),
    }


def modulate(tokens, shift_vec, scale_vec):
    values = tokens.astype(jnp.float32)
    average = lax.optimization_barrier(jnp.mean(values, axis=-1, keepdims=True))
    centred = values - average
    variance = lax.optimization_barrier(jnp.mean(centred * centred, axis=-1, keepdims=True))
    normed = centred / jnp.sqrt(variance + 1e-06)
    return (normed * (1.0 + scale_vec) + shift_vec).astype(jnp.bfloat16)

def attend(queries, key_rows, values):
    scores = jnp.einsum('nqe,nke->nqk', queries.astype(jnp.float32), key_rows.astype(jnp.float32)) / math.sqrt(queries.shape[-1])
    row_max = lax.optimization_barrier(jnp.max(scores, axis=-1, keepdims=True))
    weights = jnp.exp(scores - row_max)
    row_total = lax.optimization_barrier(jnp.sum(weights, axis=-1, keepdims=True))
    rounded = lax.optimization_barrier(weights.astype(jnp.bfloat16))
    attended = jnp.einsum('nqk,nke->nqe', rounded.astype(jnp.float32), values.astype(jnp.float32))
    return (attended / row_total).astype(jnp.bfloat16)

def spatial(clip, modulation, w_qkv, w_out):

    def one_frame(tokens):
        normed = modulate(tokens, modulation[0], modulation[1])
        packed = jnp.dot(normed, w_qkv, preferred_element_type=jnp.float32).astype(jnp.bfloat16)
        packed = lax.optimization_barrier(packed)
        pieces = packed.reshape(S, 3, HEADS, HEAD_DIM).transpose(1, 2, 0, 3)
        attended = attend(pieces[0], pieces[1], pieces[2])
        attended = attended.transpose(1, 0, 2).reshape(S, D)
        projected = jnp.dot(attended, w_out, preferred_element_type=jnp.float32)
        return (tokens.astype(jnp.float32) + modulation[2] * projected).astype(jnp.bfloat16)
    return lax.map(one_frame, clip)

def temporal(middle, modulation, w_qkv, w_out):
    normed = modulate(middle, modulation[3], modulation[4])
    packed = jnp.dot(normed.reshape(F * S, D), w_qkv, preferred_element_type=jnp.float32).astype(jnp.bfloat16)
    packed = lax.optimization_barrier(packed)
    pieces = packed.reshape(F, S, 3, HEADS, HEAD_DIM).transpose(2, 1, 3, 0, 4).reshape(3, S * HEADS, F, HEAD_DIM)
    attended = attend(pieces[0], pieces[1], pieces[2])
    attended = attended.reshape(S, HEADS, F, HEAD_DIM).transpose(2, 0, 1, 3).reshape(F * S, D)
    projected = jnp.dot(attended, w_out, preferred_element_type=jnp.float32).reshape(F, S, D)
    return (middle.astype(jnp.float32) + modulation[5] * projected).astype(jnp.bfloat16)

def reference(clip, modulation, w_qkv_s, w_out_s, w_qkv_t, w_out_t):
    middle = spatial(clip, modulation, w_qkv_s, w_out_s)
    return temporal(middle, modulation, w_qkv_t, w_out_t)
```

```python
import functools
import math

import jax
import jax.numpy as jnp
from jax import lax
from jax.experimental import pallas as pl
from jax.experimental.pallas import tpu as pltpu
from jax.sharding import PartitionSpec as P

HEADS = 16
PAIRS = 8
HEAD_DIM = 72
PAIR_COLS = 144
WIDTH = 1152
ROWS = 448
LANES = 896
AUG = 80
QSCALE = math.log2(math.e) / math.sqrt(HEAD_DIM)
NT = (((1,), (1,)), ((), ()))
VMEM_LIMIT = 58 * 1024 * 1024


def modulate(values, shift_vec, scale_vec):
    values = values.astype(jnp.float32)
    average = jnp.mean(values, axis=-1, keepdims=True)
    centred = values - average
    variance = jnp.mean(centred * centred, axis=-1, keepdims=True)
    normed = centred * lax.rsqrt(variance + 1e-06)
    return (normed * (1.0 + scale_vec) + shift_vec).astype(jnp.bfloat16)


def key_phase(x_refs, mod_ref, wk_ref, xn_ref, k_ref):
    for i, x_ref in enumerate(x_refs):
        rows = pl.ds(i * ROWS, ROWS)
        xn_ref[rows, :] = modulate(x_ref[...], mod_ref[0:1, :], mod_ref[1:2, :])
        k_ref[rows, :] = jnp.dot(
            xn_ref[rows, :], wk_ref[...], preferred_element_type=jnp.float32
        ).astype(jnp.bfloat16)


def attend_pair(pair, xn_ref, k_ref, wvt_ref, qq_ref, tile):
    keys = xn_ref.shape[0]
    vt = lax.dot_general(wvt_ref[...], xn_ref[...], NT, preferred_element_type=jnp.float32)
    first = lax.broadcasted_iota(jnp.int32, (AUG - HEAD_DIM, keys), 0) == 0
    tail = jnp.where(first, 1.0, 0.0)
    va = jnp.concatenate([vt[:HEAD_DIM], tail], axis=0).astype(jnp.bfloat16)
    vb = jnp.concatenate([vt[HEAD_DIM:], tail], axis=0).astype(jnp.bfloat16)
    kw = k_ref[:, pl.ds(pl.multiple_of(pair * 128, 128), 256)]
    starts = list(range(0, LANES, tile))

    def score(start):
        width = min(tile, LANES - start)
        return jnp.dot(kw, qq_ref[:, start : start + width], preferred_element_type=jnp.float32)

    out = []
    ahead = score(starts[0])
    for i, start in enumerate(starts):
        scores = ahead
        if i + 1 < len(starts):
            ahead = score(starts[i + 1])
        width = scores.shape[1]
        top = jnp.max(scores, axis=0, keepdims=True)
        weights = jnp.exp2(scores - top).astype(jnp.bfloat16)
        if start + width <= ROWS:
            total = jnp.dot(va, weights, preferred_element_type=jnp.float32)
        elif start >= ROWS:
            total = jnp.dot(vb, weights, preferred_element_type=jnp.float32)
        else:
            lane = lax.broadcasted_iota(jnp.int32, (AUG, width), 1)
            total = jnp.where(
                lane < ROWS - start,
                jnp.dot(va, weights, preferred_element_type=jnp.float32),
                jnp.dot(vb, weights, preferred_element_type=jnp.float32),
            )
        out.append((start, width, total, top))
    return out


def near_kernel(tile, xo_ref, xp_ref, mod_ref, wk_ref, wqt_ref, wvt_ref, qq_ref, acc_ref, top_ref, xn_ref, k_ref):
    pair = pl.program_id(0)

    @pl.when(pair == 0)
    def _():
        key_phase((xo_ref, xp_ref), mod_ref, wk_ref, xn_ref, k_ref)

    qt = lax.dot_general(wqt_ref[...], xn_ref[0:ROWS, :], NT, preferred_element_type=jnp.float32) * QSCALE
    zero = jnp.zeros((HEAD_DIM, ROWS), jnp.float32)
    qa = jnp.concatenate([qt[:HEAD_DIM], zero], axis=0).astype(jnp.bfloat16)
    qb = jnp.concatenate([zero, qt[HEAD_DIM:]], axis=0).astype(jnp.bfloat16)
    qq_ref[...] = jnp.zeros_like(qq_ref)
    place = pl.ds(pl.multiple_of(pair * 16, 16), PAIR_COLS)
    qq_ref[place, :] = jnp.concatenate([qa, qb], axis=1)
    for start, width, total, top in attend_pair(pair, xn_ref, k_ref, wvt_ref, qq_ref, tile):
        acc_ref[:, start : start + width] = total
        top_ref[:, start : start + width] = jnp.broadcast_to(top, (8, width))


def far_kernel(
    tile, xa_ref, xb_ref, xo_ref, mod_ref, wk_ref, wvt_ref, wo_ref, qq_ref, acc_ref, top_ref, out_ref, xn_ref, k_ref, att_ref
):
    pair = pl.program_id(0)

    @pl.when(pair == 0)
    def _():
        key_phase((xa_ref, xb_ref), mod_ref, wk_ref, xn_ref, k_ref)

    parts = []
    for start, width, total, top in attend_pair(pair, xn_ref, k_ref, wvt_ref, qq_ref, tile):
        old_top = top_ref[0:1, start : start + width]
        new_top = jnp.maximum(old_top, top)
        total = total * jnp.exp2(top - new_top) + acc_ref[:, start : start + width] * jnp.exp2(old_top - new_top)
        parts.append(total[:HEAD_DIM] / total[HEAD_DIM : HEAD_DIM + 1])
    merged = jnp.concatenate(parts, axis=1)
    both = jnp.concatenate([merged[:, :ROWS], merged[:, ROWS:]], axis=0).astype(jnp.bfloat16)
    att_ref[pl.ds(pl.multiple_of(pair * PAIR_COLS, 16), PAIR_COLS), :] = both

    @pl.when(pair == PAIRS - 1)
    def _():
        projected = lax.dot_general(
            att_ref[...], wo_ref[...], (((0,), (0,)), ((), ())), preferred_element_type=jnp.float32
        )
        middle = xo_ref[...].astype(jnp.float32) + mod_ref[2:3, :] * projected
        for d in range(16):
            piece = jnp.concatenate([middle[28 * d : 28 * d + 28], jnp.zeros((4, WIDTH), jnp.float32)], axis=0)
            out_ref[d] = piece.astype(jnp.bfloat16)


def whole(shape):
    return pl.BlockSpec(shape, lambda p: (0,) * len(shape))


def near(xo, xp, mod, wk, wqt, wvt, tile=256):
    return pl.pallas_call(
        functools.partial(near_kernel, tile),
        grid=(PAIRS,),
        in_specs=[
            whole((ROWS, WIDTH)),
            whole((ROWS, WIDTH)),
            whole((6, WIDTH)),
            whole((WIDTH, WIDTH)),
            pl.BlockSpec((PAIR_COLS, WIDTH), lambda p: (p, 0)),
            pl.BlockSpec((PAIR_COLS, WIDTH), lambda p: (p, 0)),
        ],
        out_specs=[
            pl.BlockSpec((None, 256, LANES), lambda p: (p, 0, 0)),
            pl.BlockSpec((None, AUG, LANES), lambda p: (p, 0, 0)),
            pl.BlockSpec((None, 8, LANES), lambda p: (p, 0, 0)),
        ],
        out_shape=[
            jax.ShapeDtypeStruct((PAIRS, 256, LANES), jnp.bfloat16),
            jax.ShapeDtypeStruct((PAIRS, AUG, LANES), jnp.float32),
            jax.ShapeDtypeStruct((PAIRS, 8, LANES), jnp.float32),
        ],
        scratch_shapes=[pltpu.VMEM((2 * ROWS, WIDTH), jnp.bfloat16), pltpu.VMEM((2 * ROWS, WIDTH), jnp.bfloat16)],
        compiler_params=pltpu.CompilerParams(vmem_limit_bytes=VMEM_LIMIT),
        cost_estimate=pl.CostEstimate(flops=20_000_000_000, bytes_accessed=20_000_000, transcendentals=6_400_000),
        name="near_tokens",
    )(xo, xp, mod, wk, wqt, wvt)


def far(xa, xb, xo, mod, wk, wvt, wo, qq, acc, top, tile=256):
    return pl.pallas_call(
        functools.partial(far_kernel, tile),
        grid=(PAIRS,),
        in_specs=[
            whole((ROWS, WIDTH)),
            whole((ROWS, WIDTH)),
            whole((ROWS, WIDTH)),
            whole((6, WIDTH)),
            whole((WIDTH, WIDTH)),
            pl.BlockSpec((PAIR_COLS, WIDTH), lambda p: (p, 0)),
            whole((WIDTH, WIDTH)),
            pl.BlockSpec((None, 256, LANES), lambda p: (p, 0, 0)),
            pl.BlockSpec((None, AUG, LANES), lambda p: (p, 0, 0)),
            pl.BlockSpec((None, 8, LANES), lambda p: (p, 0, 0)),
        ],
        out_specs=whole((16, 32, WIDTH)),
        out_shape=jax.ShapeDtypeStruct((16, 32, WIDTH), jnp.bfloat16),
        scratch_shapes=[
            pltpu.VMEM((2 * ROWS, WIDTH), jnp.bfloat16),
            pltpu.VMEM((2 * ROWS, WIDTH), jnp.bfloat16),
            pltpu.VMEM((WIDTH, ROWS), jnp.bfloat16),
        ],
        compiler_params=pltpu.CompilerParams(vmem_limit_bytes=VMEM_LIMIT),
        cost_estimate=pl.CostEstimate(flops=20_000_000_000, bytes_accessed=20_000_000, transcendentals=6_400_000),
        name="far_tokens",
    )(xa, xb, xo, mod, wk, wvt, wo, qq, acc, top)


def temporal_kernel(mid_ref, mod_ref, w_ref, wo_ref, out_ref, qkv_ref, att_ref):
    rows = 512
    x = mid_ref[...].reshape(rows, WIDTH)
    xn = modulate(x, mod_ref[3:4, :], mod_ref[4:5, :])
    for j in range(3):
        cols = slice(j * WIDTH, (j + 1) * WIDTH)
        part = jnp.dot(xn, w_ref[:, cols], preferred_element_type=jnp.float32)
        if j == 0:
            part = part * QSCALE
        qkv_ref[:, cols] = part
    lane = lax.broadcasted_iota(jnp.int32, (1, 256), 1)
    key_token = lax.broadcasted_iota(jnp.int32, (128, 256), 1) % 8
    query_token = lax.broadcasted_iota(jnp.int32, (128, 256), 0) % 8
    same = key_token == query_token
    groups = qkv_ref[...].reshape(16, 4, 8, 3 * WIDTH)
    for g in range(4):
        block = groups[:, g].reshape(128, 3 * WIDTH).astype(jnp.bfloat16)
        outs = []
        for p in range(PAIRS):
            win = slice(128 * p, 128 * p + 256)
            q = block[:, win]
            k = block[:, WIDTH + 128 * p : WIDTH + 128 * p + 256]
            v = block[:, 2 * WIDTH + 128 * p : 2 * WIDTH + 128 * p + 256]
            head_a = (lane >= 16 * p) & (lane < 16 * p + 72)
            head_b = (lane >= 16 * p + 72) & (lane < 16 * p + 144)
            zero = jnp.zeros_like(k)
            kk = jnp.concatenate([jnp.where(head_a, k, zero), jnp.where(head_b, k, zero)], axis=0)
            scores = lax.dot_general(q, kk, NT, preferred_element_type=jnp.float32)
            scores = jnp.where(same, scores, -1e30)
            top_a = jnp.max(scores[:, :128], axis=1, keepdims=True)
            top_b = jnp.max(scores[:, 128:], axis=1, keepdims=True)
            wa = jnp.where(same[:, :128], jnp.exp2(scores[:, :128] - top_a), 0.0)
            wb = jnp.where(same[:, 128:], jnp.exp2(scores[:, 128:] - top_b), 0.0)
            sum_a = jnp.sum(wa, axis=1, keepdims=True)
            sum_b = jnp.sum(wb, axis=1, keepdims=True)
            ww = jnp.concatenate([wa, wb], axis=1).astype(jnp.bfloat16)
            vv = jnp.concatenate([jnp.where(head_a, v, zero), jnp.where(head_b, v, zero)], axis=0)
            total = jnp.dot(ww, vv, preferred_element_type=jnp.float32)
            outs.append(jnp.where(head_a, total / sum_a, total / sum_b))
        tiles = []
        for t in range(9):
            left = outs[t][:, :128] if t < PAIRS else None
            right = outs[t - 1][:, 128:] if t > 0 else None
            if left is None:
                tiles.append(right)
            elif right is None:
                tiles.append(left)
            else:
                tiles.append(jnp.where(lane[:, :128] < 16 * t, right, left))
        merged = jnp.concatenate(tiles, axis=1).astype(jnp.bfloat16)
        att_ref[g * 128 : g * 128 + 128, :] = merged
    projected = jnp.dot(att_ref[...], wo_ref[...], preferred_element_type=jnp.float32)
    for g in range(4):
        piece = projected[g * 128 : g * 128 + 128].reshape(16, 8, WIDTH)
        rest = mid_ref[...].astype(jnp.float32)[:, 8 * g : 8 * g + 8, :]
        qkv_ref[:, 0:WIDTH].reshape(16, 32, WIDTH)
        done = rest + mod_ref[5:6, :][None] * piece
        qkv_ref[g * 128 : g * 128 + 128, 0:WIDTH] = done.reshape(128, WIDTH)
    final = qkv_ref[:, 0:WIDTH].reshape(4, 16, 8, WIDTH)
    for f in range(16):
        out_ref[f] = jnp.concatenate([final[g, f] for g in range(4)], axis=0).astype(jnp.bfloat16)


def temporal(mid, mod, w, wo):
    return pl.pallas_call(
        temporal_kernel,
        out_shape=jax.ShapeDtypeStruct((16, 32, WIDTH), jnp.bfloat16),
        in_specs=[pl.BlockSpec(memory_space=pltpu.VMEM)] * 4,
        out_specs=pl.BlockSpec(memory_space=pltpu.VMEM),
        scratch_shapes=[pltpu.VMEM((512, 3 * WIDTH), jnp.float32), pltpu.VMEM((512, WIDTH), jnp.bfloat16)],
        compiler_params=pltpu.CompilerParams(vmem_limit_bytes=VMEM_LIMIT),
        cost_estimate=pl.CostEstimate(flops=6_000_000_000, bytes_accessed=14_000_000, transcendentals=1_000_000),
        name="temporal_block",
    )(mid, mod, w, wo)


def local(clip, modulation, w_qkv_s, w_out_s, w_qkv_t, w_out_t):
    own = clip[0]
    swap_chip = [(0, 2), (1, 3), (2, 0), (3, 1)]
    swap_core = [(0, 1), (1, 0), (2, 3), (3, 2)]
    there = lax.ppermute(own, "head", swap_chip)
    peer = lax.ppermute(own, "head", swap_core)
    wk = w_qkv_s[:, WIDTH : 2 * WIDTH]
    wqt = w_qkv_s[:, :WIDTH].T
    wvt = w_qkv_s[:, 2 * WIDTH :].T
    qq, acc, top = near(own, peer, modulation, wk, wqt, wvt)
    there_peer = lax.ppermute(there, "head", swap_core)
    middle = far(there, there_peer, own, modulation, wk, wvt, w_out_s, qq, acc, top)
    block = lax.all_to_all(middle, "tm", split_axis=0, concat_axis=0, tiled=True)
    done = temporal(block, modulation, w_qkv_t, w_out_t)
    back = lax.all_to_all(done, "tm", split_axis=0, concat_axis=0, tiled=True)
    return back[:, :28, :].reshape(1, ROWS, WIDTH)


def solution(mesh):
    placed = (P(("dp", "tm"), "head", None), P("dp", None), P(), P(), P(), P())
    return jax.shard_map(
        local, mesh=mesh, in_specs=placed, out_specs=P(("dp", "tm"), "head", None), check_vma=False
    )
```

```python
import math

import jax
import jax.numpy as jnp
from jax import lax
from jax.experimental import pallas as pl
from jax.experimental.pallas import tpu as pltpu
from jax.sharding import PartitionSpec as P

HEADS = 16
HEAD_DIM = 72
WIDTH = 1152
ROWS = 448
LANES = 896
WINDOW = 640
HALF_COLS = 576
AUG = 80
PADDED = 512
TILE = 512
QSCALE = math.log2(math.e) / math.sqrt(HEAD_DIM)
NT = (((1,), (1,)), ((), ()))
TN = (((0,), (0,)), ((), ()))
BF16 = jnp.bfloat16
F32 = jnp.float32
VMEM = pl.BlockSpec(memory_space=pltpu.VMEM)
SMEM = pl.BlockSpec(memory_space=pltpu.SMEM)
HBM = pl.BlockSpec(memory_space=pl.ANY)


def params():
    return pltpu.CompilerParams(vmem_limit_bytes=48 * 1024 * 1024)


def modulate(values, shift_vec, scale_vec):
    values = values.astype(F32)
    average = jnp.mean(values, axis=-1, keepdims=True)
    centred = values - average
    variance = jnp.mean(centred * centred, axis=-1, keepdims=True)
    normed = centred * lax.rsqrt(variance + 1e-06)
    return (normed * (1.0 + scale_vec) + shift_vec).astype(BF16)


def window_copies(w_hbm, w_ref, sems, core, thirds):
    copies = []
    for i, third in enumerate(thirds):
        start = pl.multiple_of(third * WIDTH + core * 512, 128)
        copies.append(
            pltpu.make_async_copy(
                w_hbm.at[:, pl.ds(start, WINDOW)], w_ref.at[:, i * WINDOW : (i + 1) * WINDOW], sems.at[i]
            )
        )
    return copies


def head_window(head, core):
    offset = head * HEAD_DIM + core * 64
    start = pl.multiple_of(jnp.minimum(offset // 128, 3) * 128, 128)
    return offset, start, offset - start


def attend_head(head, core, q_ref, keys_values, old):
    offset, start, inside = head_window(head, core)
    lane = lax.broadcasted_iota(jnp.int32, (1, 256), 1)
    mine = (lane >= inside) & (lane < inside + HEAD_DIM)
    queries = jnp.where(mine, q_ref[:, pl.ds(start, 256)], jnp.zeros((), BF16))
    keys, values = [], []
    for k_ref, vt_ref in keys_values:
        keys.append(k_ref[:, pl.ds(start, 256)])
        count = k_ref.shape[0]
        first = lax.broadcasted_iota(jnp.int32, (AUG - HEAD_DIM, count), 0) == 0
        vt = vt_ref[pl.ds(pl.multiple_of(offset, 8), HEAD_DIM), :]
        values.append(jnp.concatenate([vt, jnp.where(first, 1.0, 0.0)], axis=0).astype(BF16))
    starts = list(range(0, LANES, TILE))

    def score(s):
        part = queries[s : min(s + TILE, LANES)]
        return [lax.dot_general(k, part, NT, preferred_element_type=F32) for k in keys]

    out = []
    ahead = score(starts[0])
    for i, s in enumerate(starts):
        scores = ahead
        if i + 1 < len(starts):
            ahead = score(starts[i + 1])
        top = jnp.max(scores[0], axis=0, keepdims=True)
        for more in scores[1:]:
            top = jnp.maximum(top, jnp.max(more, axis=0, keepdims=True))
        total = None
        if old is not None:
            acc_ref, top_ref = old
            lanes = slice(s, s + scores[0].shape[1])
            before = top_ref[head, 0:1, lanes]
            top = jnp.maximum(top, before)
            total = acc_ref[head, :, lanes] * jnp.exp2(before - top)
        for value, part in zip(values, scores):
            term = jnp.dot(value, jnp.exp2(part - top).astype(BF16), preferred_element_type=F32)
            total = term if total is None else total + term
        out.append((s, total, top))
    return out


def near_kernel(core_ref, xo_ref, xp_ref, mod_ref, w_hbm, q_ref, acc_ref, top_ref, xn_ref, w_ref, k_ref, vt_ref, sems):
    core = core_ref[0]
    copies = window_copies(w_hbm, w_ref, sems, core, (0, 1, 2))
    for copy in copies:
        copy.start()
    xn_ref[0:ROWS, :] = modulate(xo_ref[...], mod_ref[0:1, :], mod_ref[1:2, :])
    xn_ref[ROWS:, :] = modulate(xp_ref[...], mod_ref[0:1, :], mod_ref[1:2, :])
    for copy in copies:
        copy.wait()
    packed = jnp.dot(xn_ref[...], w_ref[...], preferred_element_type=F32)
    q_ref[...] = (packed[:, :WINDOW] * QSCALE).astype(BF16)
    k_ref[...] = packed[:, WINDOW : 2 * WINDOW].astype(BF16)
    vt_ref[...] = packed[:, 2 * WINDOW :].T

    def pair(p, carry):
        for h in range(2):
            head = 2 * p + h
            for s, total, top in attend_head(head, core, q_ref, ((k_ref, vt_ref),), None):
                width = total.shape[1]
                acc_ref[head, :, s : s + width] = total
                top_ref[head, :, s : s + width] = jnp.broadcast_to(top, (8, width))
        return carry

    lax.fori_loop(0, 4, pair, 0)


def near(core, xo, xp, mod, w):
    return pl.pallas_call(
        near_kernel,
        in_specs=[SMEM, VMEM, VMEM, VMEM, HBM],
        out_specs=[VMEM] * 3,
        out_shape=[
            jax.ShapeDtypeStruct((LANES, WINDOW), BF16),
            jax.ShapeDtypeStruct((8, AUG, LANES), F32),
            jax.ShapeDtypeStruct((8, 8, LANES), F32),
        ],
        scratch_shapes=[
            pltpu.VMEM((LANES, WIDTH), BF16),
            pltpu.VMEM((WIDTH, 3 * WINDOW), BF16),
            pltpu.VMEM((LANES, WINDOW), BF16),
            pltpu.VMEM((WINDOW, LANES), F32),
            pltpu.SemaphoreType.DMA((3,)),
        ],
        compiler_params=params(),
        cost_estimate=pl.CostEstimate(flops=20_000_000_000, bytes_accessed=10_000_000, transcendentals=6_400_000),
        name="near_tokens",
    )(core, xo, xp, mod, w)


def project_kernel(core_ref, x_ref, mod_ref, w_hbm, k_ref, vt_ref, w_ref, sems):
    copies = window_copies(w_hbm, w_ref, sems, core_ref[0], (1, 2))
    for copy in copies:
        copy.start()
    xn = modulate(x_ref[...], mod_ref[0:1, :], mod_ref[1:2, :])
    for copy in copies:
        copy.wait()
    packed = jnp.dot(xn, w_ref[...], preferred_element_type=F32)
    k_ref[...] = packed[:, :WINDOW].astype(BF16)
    vt_ref[...] = packed[:, WINDOW:].T


def project(core, x, mod, w):
    return pl.pallas_call(
        project_kernel,
        in_specs=[SMEM, VMEM, VMEM, HBM],
        out_specs=[VMEM] * 2,
        out_shape=[jax.ShapeDtypeStruct((ROWS, WINDOW), BF16), jax.ShapeDtypeStruct((WINDOW, ROWS), F32)],
        scratch_shapes=[pltpu.VMEM((WIDTH, 2 * WINDOW), BF16), pltpu.SemaphoreType.DMA((2,))],
        compiler_params=params(),
        cost_estimate=pl.CostEstimate(flops=2_000_000_000, bytes_accessed=6_000_000, transcendentals=0),
        name="far_keys",
    )(core, x, mod, w)


def far_kernel(
    core_ref, x_ref, mod_ref, w_hbm, k1_ref, vt1_ref, q_ref, acc_ref, top_ref, own_ref, peer_ref, w_ref, k_ref, vt_ref, sems
):
    core = core_ref[0]
    project_kernel(core_ref, x_ref, mod_ref, w_hbm, k_ref, vt_ref, w_ref, sems)

    def pair(p, carry):
        halves = []
        for h in range(2):
            parts = attend_head(
                2 * p + h, core, q_ref, ((k1_ref, vt1_ref), (k_ref, vt_ref)), (acc_ref, top_ref)
            )
            halves.append(
                jnp.concatenate([t[:HEAD_DIM] / t[HEAD_DIM : HEAD_DIM + 1] for _, t, _ in parts], axis=1)
            )
        both = jnp.concatenate(halves, axis=0)
        rows = pl.ds(pl.multiple_of(p * 2 * HEAD_DIM, 16), 2 * HEAD_DIM)
        own_ref[rows, :] = both[:, :ROWS].astype(BF16)
        peer_ref[rows, :] = jnp.concatenate(
            [both[:, ROWS:], jnp.zeros((2 * HEAD_DIM, PADDED - ROWS), F32)], axis=1
        ).astype(BF16)
        return carry

    lax.fori_loop(0, 4, pair, 0)


def far(core, x, mod, w, k1, vt1, q, acc, top):
    return pl.pallas_call(
        far_kernel,
        in_specs=[SMEM, VMEM, VMEM, HBM] + [VMEM] * 5,
        out_specs=[VMEM] * 2,
        out_shape=[jax.ShapeDtypeStruct((HALF_COLS, ROWS), BF16), jax.ShapeDtypeStruct((HALF_COLS, PADDED), BF16)],
        scratch_shapes=[
            pltpu.VMEM((WIDTH, 2 * WINDOW), BF16),
            pltpu.VMEM((ROWS, WINDOW), BF16),
            pltpu.VMEM((WINDOW, ROWS), F32),
            pltpu.SemaphoreType.DMA((2,)),
        ],
        compiler_params=params(),
        cost_estimate=pl.CostEstimate(flops=18_000_000_000, bytes_accessed=10_000_000, transcendentals=6_400_000),
        name="far_tokens",
    )(core, x, mod, w, k1, vt1, q, acc, top)


def join_kernel(core_ref, mine_ref, other_ref, x_ref, mod_ref, wo_ref, out_ref, att_ref):
    core = core_ref[0]
    att_ref[pl.ds(pl.multiple_of(core * HALF_COLS, 16), HALF_COLS), :] = mine_ref[...]
    att_ref[pl.ds(pl.multiple_of((1 - core) * HALF_COLS, 16), HALF_COLS), :] = other_ref[:, :ROWS]
    projected = lax.dot_general(att_ref[...], wo_ref[...], TN, preferred_element_type=F32)
    middle = x_ref[...].astype(F32) + mod_ref[2:3, :] * projected
    for d in range(16):
        piece = jnp.concatenate([middle[28 * d : 28 * d + 28], jnp.zeros((4, WIDTH), F32)], axis=0)
        out_ref[d] = piece.astype(BF16)


def join(core, mine, other, x, mod, wo):
    return pl.pallas_call(
        join_kernel,
        in_specs=[SMEM] + [VMEM] * 5,
        out_specs=VMEM,
        out_shape=jax.ShapeDtypeStruct((16, 32, WIDTH), BF16),
        scratch_shapes=[pltpu.VMEM((WIDTH, ROWS), BF16)],
        compiler_params=params(),
        cost_estimate=pl.CostEstimate(flops=1_200_000_000, bytes_accessed=6_000_000, transcendentals=0),
        name="spatial_out",
    )(core, mine, other, x, mod, wo)


def temporal_kernel(mid_ref, mod_ref, w_hbm, wo_hbm, out_ref, x_ref, w_ref, wo_ref, q_ref, k_ref, vt_ref, att_ref, sems):
    copies = [
        pltpu.make_async_copy(w_hbm.at[:, i * WIDTH : (i + 1) * WIDTH], w_ref.at[:, i * WIDTH : (i + 1) * WIDTH], sems.at[i])
        for i in range(3)
    ]
    copies.append(pltpu.make_async_copy(wo_hbm, wo_ref, sems.at[3]))
    for copy in copies:
        copy.start()
    for g in range(4):
        for f in range(16):
            x_ref[(g * 16 + f) * 8 : (g * 16 + f + 1) * 8, :] = mid_ref[f].astype(F32)[8 * g : 8 * g + 8]
    xn = modulate(x_ref[...], mod_ref[3:4, :], mod_ref[4:5, :])
    for copy in copies[:3]:
        copy.wait()
    packed = jnp.dot(xn, w_ref[...], preferred_element_type=F32)
    q_ref[...] = (packed[:, :WIDTH] * QSCALE).astype(BF16)
    k_ref[...] = packed[:, WIDTH : 2 * WIDTH].astype(BF16)
    vt_ref[...] = packed[:, 2 * WIDTH :].T
    lane = lax.broadcasted_iota(jnp.int32, (1, 256), 1)
    same = lax.broadcasted_iota(jnp.int32, (128, 256), 0) % 8 == lax.broadcasted_iota(jnp.int32, (128, 256), 1) % 8
    tail = jnp.where(lax.broadcasted_iota(jnp.int32, (AUG - HEAD_DIM, 128), 0) == 0, 1.0, 0.0)

    for g in range(4):
        rows = slice(g * 128, (g + 1) * 128)
        for p in range(8):
            inside = 16 * p
            window = slice(128 * p, 128 * p + 256)
            q = q_ref[rows, window]
            none = jnp.zeros((), BF16)
            first = jnp.where((lane >= inside) & (lane < inside + HEAD_DIM), q, none)
            second = jnp.where((lane >= inside + HEAD_DIM) & (lane < inside + 2 * HEAD_DIM), q, none)
            queries = jnp.concatenate([first, second], axis=0)
            scores = lax.dot_general(k_ref[rows, window], queries, NT, preferred_element_type=F32)
            scores = jnp.where(same, scores, -1e30)
            top = jnp.max(scores, axis=0, keepdims=True)
            weights = jnp.exp2(scores - top).astype(BF16)
            at = 2 * HEAD_DIM * p
            values = jnp.concatenate(
                [vt_ref[at : at + HEAD_DIM, rows], tail, vt_ref[at + HEAD_DIM : at + 2 * HEAD_DIM, rows], tail], axis=0
            ).astype(BF16)
            total = jnp.dot(values, weights, preferred_element_type=F32)
            a = total[:HEAD_DIM, :128] / total[HEAD_DIM : HEAD_DIM + 1, :128]
            b = total[AUG : AUG + HEAD_DIM, 128:] / total[AUG + HEAD_DIM : AUG + HEAD_DIM + 1, 128:]
            att_ref[at : at + 2 * HEAD_DIM, rows] = jnp.concatenate([a, b], axis=0).astype(BF16)
    copies[3].wait()
    projected = lax.dot_general(att_ref[...], wo_ref[...], TN, preferred_element_type=F32)
    x_ref[...] = x_ref[...] + mod_ref[5:6, :] * projected
    for f in range(16):
        pieces = [x_ref[(g * 16 + f) * 8 : (g * 16 + f + 1) * 8, :] for g in range(4)]
        out_ref[f] = jnp.concatenate(pieces, axis=0).astype(BF16)


def temporal(mid, mod, w, wo):
    return pl.pallas_call(
        temporal_kernel,
        in_specs=[VMEM, VMEM, HBM, HBM],
        out_specs=VMEM,
        out_shape=jax.ShapeDtypeStruct((16, 32, WIDTH), BF16),
        scratch_shapes=[
            pltpu.VMEM((512, WIDTH), F32),
            pltpu.VMEM((WIDTH, 3 * WIDTH), BF16),
            pltpu.VMEM((WIDTH, WIDTH), BF16),
            pltpu.VMEM((512, WIDTH), BF16),
            pltpu.VMEM((512, WIDTH), BF16),
            pltpu.VMEM((WIDTH, 512), F32),
            pltpu.VMEM((WIDTH, 512), BF16),
            pltpu.SemaphoreType.DMA((4,)),
        ],
        compiler_params=params(),
        cost_estimate=pl.CostEstimate(flops=6_000_000_000, bytes_accessed=14_000_000, transcendentals=1_000_000),
        name="temporal_block",
    )(mid, mod, w, wo)


def local(clip, modulation, w_qkv_s, w_out_s, w_qkv_t, w_out_t):
    own = clip[0]
    core = (lax.axis_index("head") % 2).astype(jnp.int32).reshape(1)
    swap_chip = [(0, 2), (1, 3), (2, 0), (3, 1)]
    swap_core = [(0, 1), (1, 0), (2, 3), (3, 2)]
    peer = lax.ppermute(own, "head", swap_core)
    there = lax.ppermute(own, "head", swap_chip)
    q, acc, top = near(core, own, peer, modulation, w_qkv_s)
    there, q = lax.optimization_barrier((there, q))
    k1, vt1 = project(core, there, modulation, w_qkv_s)
    there_peer = lax.ppermute(there, "head", swap_core)
    mine, theirs = far(core, there_peer, modulation, w_qkv_s, k1, vt1, q, acc, top)
    other = lax.ppermute(theirs, "head", swap_core)
    middle = join(core, mine, other, own, modulation, w_out_s)
    block = lax.all_to_all(middle, "tm", split_axis=0, concat_axis=0, tiled=True)
    done = temporal(block, modulation, w_qkv_t, w_out_t)
    back = lax.all_to_all(done, "tm", split_axis=0, concat_axis=0, tiled=True)
    return back[:, :28, :].reshape(1, ROWS, WIDTH)


def solution(mesh):
    placed = (P(("dp", "tm"), "head", None), P("dp", None), P(), P(), P(), P())
    return jax.shard_map(
        local, mesh=mesh, in_specs=placed, out_specs=P(("dp", "tm"), "head", None), check_vma=False
    )
```

```python
import math

import jax
import jax.numpy as jnp
from jax import lax
from jax.experimental import pallas as pl
from jax.experimental.pallas import tpu as pltpu
from jax.sharding import PartitionSpec as P

HEADS = 16
HEAD_DIM = 72
WIDTH = 1152
ROWS = 448
LANES = 896
WINDOW = 640
HALF_COLS = 576
AUG = 80
PADDED = 512
TILE = 512
QSCALE = math.log2(math.e) / math.sqrt(HEAD_DIM)
NT = (((1,), (1,)), ((), ()))
TN = (((0,), (0,)), ((), ()))
BF16 = jnp.bfloat16
F32 = jnp.float32
VMEM = pl.BlockSpec(memory_space=pltpu.VMEM)
SMEM = pl.BlockSpec(memory_space=pltpu.SMEM)
HBM = pl.BlockSpec(memory_space=pl.ANY)


def params(mebibytes):
    return pltpu.CompilerParams(vmem_limit_bytes=mebibytes * 1024 * 1024)


def modulate(values, shift_vec, scale_vec):
    values = values.astype(F32)
    average = jnp.mean(values, axis=-1, keepdims=True)
    centred = values - average
    variance = jnp.mean(centred * centred, axis=-1, keepdims=True)
    normed = centred * lax.rsqrt(variance + 1e-06)
    return (normed * (1.0 + scale_vec) + shift_vec).astype(BF16)


def window_copies(w_hbm, w_ref, sems, core, thirds):
    copies = []
    for i, third in enumerate(thirds):
        start = pl.multiple_of(third * WIDTH + core * 512, 128)
        copies.append(
            pltpu.make_async_copy(
                w_hbm.at[:, pl.ds(start, WINDOW)], w_ref.at[:, i * WINDOW : (i + 1) * WINDOW], sems.at[i]
            )
        )
    return copies


def head_window(head, core):
    offset = head * HEAD_DIM + core * 64
    start = pl.multiple_of(jnp.minimum(offset // 128, 3) * 128, 128)
    return offset, start, offset - start


def attend_head(head, core, q_ref, keys_values, old):
    offset, start, inside = head_window(head, core)
    lane = lax.broadcasted_iota(jnp.int32, (1, 256), 1)
    mine = (lane >= inside) & (lane < inside + HEAD_DIM)
    queries = jnp.where(mine, q_ref[:, pl.ds(start, 256)], jnp.zeros((), BF16))
    keys, values = [], []
    for k_ref, vt_ref in keys_values:
        keys.append(k_ref[:, pl.ds(start, 256)])
        count = k_ref.shape[0]
        first = lax.broadcasted_iota(jnp.int32, (AUG - HEAD_DIM, count), 0) == 0
        vt = vt_ref[pl.ds(pl.multiple_of(offset, 8), HEAD_DIM), :]
        values.append(jnp.concatenate([vt, jnp.where(first, 1.0, 0.0)], axis=0).astype(BF16))
    starts = list(range(0, LANES, TILE))

    def score(s):
        part = queries[s : min(s + TILE, LANES)]
        return [lax.dot_general(k, part, NT, preferred_element_type=F32) for k in keys]

    out = []
    ahead = score(starts[0])
    for i, s in enumerate(starts):
        scores = ahead
        if i + 1 < len(starts):
            ahead = score(starts[i + 1])
        top = jnp.max(scores[0], axis=0, keepdims=True)
        for more in scores[1:]:
            top = jnp.maximum(top, jnp.max(more, axis=0, keepdims=True))
        total = None
        if old is not None:
            acc_ref, top_ref = old
            lanes = slice(s, s + scores[0].shape[1])
            before = top_ref[head, 0:1, lanes]
            top = jnp.maximum(top, before)
            total = acc_ref[head, :, lanes] * jnp.exp2(before - top)
        for value, part in zip(values, scores):
            term = jnp.dot(value, jnp.exp2(part - top).astype(BF16), preferred_element_type=F32)
            total = term if total is None else total + term
        out.append((s, total, top))
    return out


def near_kernel(core_ref, xo_ref, xp_ref, mod_ref, w_hbm, q_ref, acc_ref, top_ref, xn_ref, w_ref, k_ref, vt_ref, sems):
    core = core_ref[0]
    copies = window_copies(w_hbm, w_ref, sems, core, (0, 1, 2))
    for copy in copies:
        copy.start()
    xn_ref[0:ROWS, :] = modulate(xo_ref[...], mod_ref[0:1, :], mod_ref[1:2, :])
    xn_ref[ROWS:, :] = modulate(xp_ref[...], mod_ref[0:1, :], mod_ref[1:2, :])
    for copy in copies:
        copy.wait()
    packed = jnp.dot(xn_ref[...], w_ref[...], preferred_element_type=F32)
    q_ref[...] = (packed[:, :WINDOW] * QSCALE).astype(BF16)
    k_ref[...] = packed[:, WINDOW : 2 * WINDOW].astype(BF16)
    vt_ref[...] = packed[:, 2 * WINDOW :].T

    def pair(p, carry):
        for h in range(2):
            head = 2 * p + h
            for s, total, top in attend_head(head, core, q_ref, ((k_ref, vt_ref),), None):
                width = total.shape[1]
                acc_ref[head, :, s : s + width] = total
                top_ref[head, :, s : s + width] = jnp.broadcast_to(top, (8, width))
        return carry

    lax.fori_loop(0, 4, pair, 0)


def near(core, xo, xp, mod, w):
    return pl.pallas_call(
        near_kernel,
        in_specs=[SMEM, VMEM, VMEM, VMEM, HBM],
        out_specs=[VMEM] * 3,
        out_shape=[
            jax.ShapeDtypeStruct((LANES, WINDOW), BF16),
            jax.ShapeDtypeStruct((8, AUG, LANES), F32),
            jax.ShapeDtypeStruct((8, 8, LANES), F32),
        ],
        scratch_shapes=[
            pltpu.VMEM((LANES, WIDTH), BF16),
            pltpu.VMEM((WIDTH, 3 * WINDOW), BF16),
            pltpu.VMEM((LANES, WINDOW), BF16),
            pltpu.VMEM((WINDOW, LANES), F32),
            pltpu.SemaphoreType.DMA((3,)),
        ],
        compiler_params=params(36),
        cost_estimate=pl.CostEstimate(flops=20_000_000_000, bytes_accessed=10_000_000, transcendentals=6_400_000),
        name="near_tokens",
    )(core, xo, xp, mod, w)


def project_kernel(core_ref, x_ref, mod_ref, w_hbm, k_ref, vt_ref, w_ref, sems):
    copies = window_copies(w_hbm, w_ref, sems, core_ref[0], (1, 2))
    for copy in copies:
        copy.start()
    xn = modulate(x_ref[...], mod_ref[0:1, :], mod_ref[1:2, :])
    for copy in copies:
        copy.wait()
    packed = jnp.dot(xn, w_ref[...], preferred_element_type=F32)
    k_ref[...] = packed[:, :WINDOW].astype(BF16)
    vt_ref[...] = packed[:, WINDOW:].T


def project(core, x, mod, w):
    return pl.pallas_call(
        project_kernel,
        in_specs=[SMEM, VMEM, VMEM, HBM],
        out_specs=[VMEM] * 2,
        out_shape=[jax.ShapeDtypeStruct((ROWS, WINDOW), BF16), jax.ShapeDtypeStruct((WINDOW, ROWS), F32)],
        scratch_shapes=[pltpu.VMEM((WIDTH, 2 * WINDOW), BF16), pltpu.SemaphoreType.DMA((2,))],
        compiler_params=params(16),
        cost_estimate=pl.CostEstimate(flops=2_000_000_000, bytes_accessed=6_000_000, transcendentals=0),
        name="far_keys",
    )(core, x, mod, w)


def far_kernel(
    core_ref, x_ref, mod_ref, w_hbm, k1_ref, vt1_ref, q_ref, acc_ref, top_ref, own_ref, peer_ref, w_ref, k_ref, vt_ref, sems
):
    core = core_ref[0]
    project_kernel(core_ref, x_ref, mod_ref, w_hbm, k_ref, vt_ref, w_ref, sems)

    def pair(p, carry):
        halves = []
        for h in range(2):
            parts = attend_head(
                2 * p + h, core, q_ref, ((k1_ref, vt1_ref), (k_ref, vt_ref)), (acc_ref, top_ref)
            )
            halves.append(
                jnp.concatenate([t[:HEAD_DIM] / t[HEAD_DIM : HEAD_DIM + 1] for _, t, _ in parts], axis=1)
            )
        both = jnp.concatenate(halves, axis=0)
        rows = pl.ds(pl.multiple_of(p * 2 * HEAD_DIM, 16), 2 * HEAD_DIM)
        own_ref[rows, :] = both[:, :ROWS].astype(BF16)
        peer_ref[rows, :] = jnp.concatenate(
            [both[:, ROWS:], jnp.zeros((2 * HEAD_DIM, PADDED - ROWS), F32)], axis=1
        ).astype(BF16)
        return carry

    lax.fori_loop(0, 4, pair, 0)


def far(core, x, mod, w, k1, vt1, q, acc, top):
    return pl.pallas_call(
        far_kernel,
        in_specs=[SMEM, VMEM, VMEM, HBM] + [VMEM] * 5,
        out_specs=[VMEM] * 2,
        out_shape=[jax.ShapeDtypeStruct((HALF_COLS, ROWS), BF16), jax.ShapeDtypeStruct((HALF_COLS, PADDED), BF16)],
        scratch_shapes=[
            pltpu.VMEM((WIDTH, 2 * WINDOW), BF16),
            pltpu.VMEM((ROWS, WINDOW), BF16),
            pltpu.VMEM((WINDOW, ROWS), F32),
            pltpu.SemaphoreType.DMA((2,)),
        ],
        compiler_params=params(36),
        cost_estimate=pl.CostEstimate(flops=18_000_000_000, bytes_accessed=10_000_000, transcendentals=6_400_000),
        name="far_tokens",
    )(core, x, mod, w, k1, vt1, q, acc, top)


def join_kernel(core_ref, mine_ref, other_ref, x_ref, mod_ref, wo_ref, out_ref, att_ref):
    core = core_ref[0]
    att_ref[pl.ds(pl.multiple_of(core * HALF_COLS, 16), HALF_COLS), :] = mine_ref[...]
    att_ref[pl.ds(pl.multiple_of((1 - core) * HALF_COLS, 16), HALF_COLS), :] = other_ref[:, :ROWS]
    projected = lax.dot_general(att_ref[...], wo_ref[...], TN, preferred_element_type=F32)
    middle = x_ref[...].astype(F32) + mod_ref[2:3, :] * projected
    for d in range(16):
        piece = jnp.concatenate([middle[28 * d : 28 * d + 28], jnp.zeros((4, WIDTH), F32)], axis=0)
        out_ref[d] = piece.astype(BF16)


def join(core, mine, other, x, mod, wo):
    return pl.pallas_call(
        join_kernel,
        in_specs=[SMEM] + [VMEM] * 5,
        out_specs=VMEM,
        out_shape=jax.ShapeDtypeStruct((16, 32, WIDTH), BF16),
        scratch_shapes=[pltpu.VMEM((WIDTH, ROWS), BF16)],
        compiler_params=params(14),
        cost_estimate=pl.CostEstimate(flops=1_200_000_000, bytes_accessed=6_000_000, transcendentals=0),
        name="spatial_out",
    )(core, mine, other, x, mod, wo)


def temporal_kernel(mid_ref, mod_ref, w_ref, wo_ref, out_ref, x_ref, q_ref, k_ref, vt_ref, att_ref):
    for i in range(8):
        lows = []
        for f in (2 * i, 2 * i + 1):
            frame = mid_ref[f].astype(F32)
            for g in range(3):
                x_ref[(g * 16 + f) * 8 : (g * 16 + f + 1) * 8, :] = frame[8 * g : 8 * g + 8]
            lows.append(frame[24:28])
        x_ref[384 + 8 * i : 392 + 8 * i, :] = jnp.concatenate(lows, axis=0)
    xn = modulate(x_ref[...], mod_ref[3:4, :], mod_ref[4:5, :])
    packed = jnp.dot(xn, w_ref[...], preferred_element_type=F32)
    q_ref[:, ROWS:] = jnp.zeros((WIDTH, PADDED - ROWS), BF16)
    q_ref[:, :ROWS] = (packed[:, :WIDTH] * QSCALE).T.astype(BF16)
    k_ref[...] = packed[:, WIDTH : 2 * WIDTH].astype(BF16)
    vt_ref[...] = packed[:, 2 * WIDTH :].T

    row = lax.broadcasted_iota(jnp.int32, (256, 1), 0)
    none = jnp.zeros((), BF16)

    def rows_of(g):
        return slice(g * 128, min(g * 128 + 128, ROWS))

    def score(g, p):
        queries = q_ref[128 * p : 128 * p + 256, g * 128 : g * 128 + 128]
        inside = 16 * p
        first = jnp.where((row >= inside) & (row < inside + HEAD_DIM), queries, none)
        second = jnp.where((row >= inside + HEAD_DIM) & (row < inside + 2 * HEAD_DIM), queries, none)
        keys = k_ref[rows_of(g), 128 * p : 128 * p + 256]
        return jnp.dot(keys, jnp.concatenate([first, second], axis=1), preferred_element_type=F32)

    def weigh(g, scores):
        every = 8 if g < 3 else 4
        shape = scores.shape
        key_token = lax.broadcasted_iota(jnp.int32, shape, 0) % every
        same = key_token == lax.broadcasted_iota(jnp.int32, shape, 1) % every
        scores = jnp.where(same, scores, -1e30)
        top = jnp.max(scores, axis=0, keepdims=True)
        return jnp.exp2(scores - top).astype(BF16)

    def value(g, p, weights):
        at = 2 * HEAD_DIM * p
        tail = jnp.where(lax.broadcasted_iota(jnp.int32, (AUG - HEAD_DIM, weights.shape[0]), 0) == 0, 1.0, 0.0)
        first = vt_ref[at : at + HEAD_DIM, rows_of(g)]
        second = vt_ref[at + HEAD_DIM : at + 2 * HEAD_DIM, rows_of(g)]
        values = jnp.concatenate([first, tail, second, tail], axis=0).astype(BF16)
        return jnp.dot(values, weights, preferred_element_type=F32)

    def finish(g, p, total):
        at = 2 * HEAD_DIM * p
        first = total[:HEAD_DIM, :128] / total[HEAD_DIM : HEAD_DIM + 1, :128]
        second = total[AUG : AUG + HEAD_DIM, 128:] / total[AUG + HEAD_DIM : AUG + HEAD_DIM + 1, 128:]
        both = jnp.concatenate([first, second], axis=0).astype(BF16)
        att_ref[at : at + 2 * HEAD_DIM, g * 128 : g * 128 + 128] = both

    order = [(g, p) for g in range(4) for p in range(8)]
    apart = 4
    scores, totals = {}, {}
    for i in range(len(order) + 2 * apart):
        if i < len(order):
            scores[i] = score(*order[i])
        j = i - apart
        if 0 <= j < len(order):
            g, p = order[j]
            totals[j] = value(g, p, weigh(g, scores.pop(j)))
        k = i - 2 * apart
        if 0 <= k < len(order):
            finish(*order[k], totals.pop(k))

    projected = lax.dot_general(att_ref[:, :ROWS], wo_ref[...], TN, preferred_element_type=F32)
    x_ref[...] = x_ref[...] + mod_ref[5:6, :] * projected
    for f in range(16):
        pieces = [x_ref[(g * 16 + f) * 8 : (g * 16 + f + 1) * 8, :] for g in range(3)]
        last = x_ref[384 + 8 * (f // 2) : 392 + 8 * (f // 2), :]
        if f % 2:
            last = jnp.concatenate([last[4:], last[:4]], axis=0)
        out_ref[f] = jnp.concatenate(pieces + [last], axis=0).astype(BF16)


def temporal(mid, mod, w, wo):
    return pl.pallas_call(
        temporal_kernel,
        in_specs=[VMEM] * 4,
        out_specs=VMEM,
        out_shape=jax.ShapeDtypeStruct((16, 32, WIDTH), BF16),
        scratch_shapes=[
            pltpu.VMEM((ROWS, WIDTH), F32),
            pltpu.VMEM((WIDTH, PADDED), BF16),
            pltpu.VMEM((ROWS, WIDTH), BF16),
            pltpu.VMEM((WIDTH, ROWS), F32),
            pltpu.VMEM((WIDTH, PADDED), BF16),
        ],
        compiler_params=params(24),
        cost_estimate=pl.CostEstimate(flops=6_000_000_000, bytes_accessed=14_000_000, transcendentals=1_000_000),
        name="temporal_block",
    )(mid, mod, w, wo)


def local(clip, modulation, w_qkv_s, w_out_s, w_qkv_t, w_out_t):
    own = clip[0]
    core = (lax.axis_index("head") % 2).astype(jnp.int32).reshape(1)
    swap_chip = [(0, 2), (1, 3), (2, 0), (3, 1)]
    swap_core = [(0, 1), (1, 0), (2, 3), (3, 2)]
    peer = lax.ppermute(own, "head", swap_core)
    there = lax.ppermute(own, "head", swap_chip)
    q, acc, top = near(core, own, peer, modulation, w_qkv_s)
    there, q = lax.optimization_barrier((there, q))
    k1, vt1 = project(core, there, modulation, w_qkv_s)
    there_peer = lax.ppermute(there, "head", swap_core)
    mine, theirs = far(core, there_peer, modulation, w_qkv_s, k1, vt1, q, acc, top)
    other = lax.ppermute(theirs, "head", swap_core)
    middle = join(core, mine, other, own, modulation, w_out_s)
    block = lax.all_to_all(middle, "tm", split_axis=0, concat_axis=0, tiled=True)
    done = temporal(block, modulation, w_qkv_t, w_out_t)
    back = lax.all_to_all(done, "tm", split_axis=0, concat_axis=0, tiled=True)
    return back[:, :28, :].reshape(1, ROWS, WIDTH)


def solution(mesh):
    placed = (P(("dp", "tm"), "head", None), P("dp", None), P(), P(), P(), P())
    return jax.shard_map(
        local, mesh=mesh, in_specs=placed, out_specs=P(("dp", "tm"), "head", None), check_vma=False
    )
```

```python
import math

import jax
import jax.numpy as jnp
from jax import lax
from jax.experimental import pallas as pl
from jax.experimental.pallas import tpu as pltpu
from jax.sharding import PartitionSpec as P

HEADS = 16
HEAD_DIM = 72
WIDTH = 1152
ROWS = 448
LANES = 896
WINDOW = 640
HALF_COLS = 576
AUG = 80
PADDED = 512
TILE = 512
QSCALE = math.log2(math.e) / math.sqrt(HEAD_DIM)
NT = (((1,), (1,)), ((), ()))
TN = (((0,), (0,)), ((), ()))
BF16 = jnp.bfloat16
F32 = jnp.float32
VMEM = pl.BlockSpec(memory_space=pltpu.VMEM)
SMEM = pl.BlockSpec(memory_space=pltpu.SMEM)
HBM = pl.BlockSpec(memory_space=pltpu.HBM)
EXCESS = 64.0


def params(mebibytes):
    return pltpu.CompilerParams(vmem_limit_bytes=mebibytes * 1024 * 1024)


def modulate(values, shift_vec, scale_vec):
    values = values.astype(F32)
    average = jnp.mean(values, axis=-1, keepdims=True)
    centred = values - average
    variance = jnp.mean(centred * centred, axis=-1, keepdims=True)
    normed = centred * lax.rsqrt(variance + 1e-06)
    return (normed * (1.0 + scale_vec) + shift_vec).astype(BF16)


def window_copy(w_hbm, third, core, place, sem):
    start = pl.multiple_of(third * WIDTH + core * 512, 128)
    return pltpu.make_async_copy(w_hbm.at[:, pl.ds(start, WINDOW)], place, sem)


def head_window(head, core):
    offset = head * HEAD_DIM + core * 64
    start = pl.multiple_of(jnp.minimum(offset // 128, 3) * 128, 128)
    return offset, start, offset - start


def head_operands(head, core, q_ref, blocks):
    offset, start, inside = head_window(head, core)
    lane = lax.broadcasted_iota(jnp.int32, (1, 256), 1)
    mine = (lane >= inside) & (lane < inside + HEAD_DIM)
    queries = jnp.where(mine, q_ref[:, pl.ds(start, 256)], jnp.zeros((), BF16))
    keys, values = [], []
    for k_ref, vt_ref in blocks:
        keys.append(k_ref[:, pl.ds(start, 256)])
        first = lax.broadcasted_iota(jnp.int32, (AUG - HEAD_DIM, k_ref.shape[0]), 0) == 0
        vt = vt_ref[pl.ds(pl.multiple_of(offset, 8), HEAD_DIM), :]
        values.append(jnp.concatenate([vt, jnp.where(first, 1.0, 0.0)], axis=0).astype(BF16))
    return queries, keys, values


def attend_head(head, core, q_ref, blocks, old, known_top):
    queries, keys, values = head_operands(head, core, q_ref, blocks)
    starts = list(range(0, LANES, TILE))

    def score(s):
        part = queries[s : min(s + TILE, LANES)]
        return [lax.dot_general(k, part, NT, preferred_element_type=F32) for k in keys]

    out = []
    ahead = score(starts[0])
    for i, s in enumerate(starts):
        scores = ahead
        if i + 1 < len(starts):
            ahead = score(starts[i + 1])
        lanes = slice(s, s + scores[0].shape[1])
        tops = [jnp.max(part, axis=0, keepdims=True) for part in scores]
        top = tops[0]
        for more in tops[1:]:
            top = jnp.maximum(top, more)
        total = None
        reference = top
        if old is not None:
            acc_ref, top_ref = old
            before = top_ref[head, 0:1, lanes]
            total = acc_ref[head, :, lanes]
            if known_top:
                reference = before
            else:
                reference = jnp.maximum(top, before)
                total = total * jnp.exp2(before - reference)
        for value, part in zip(values, scores):
            term = jnp.dot(value, jnp.exp2(part - reference).astype(BF16), preferred_element_type=F32)
            total = term if total is None else total + term
        out.append((s, total, reference, top))
    return out


def keys_values(xn, w_ref, k_ref, vt_ref):
    packed = jnp.dot(xn, w_ref[...], preferred_element_type=F32)
    k_ref[...] = packed[:, :WINDOW].astype(BF16)
    vt_ref[...] = packed[:, WINDOW:].T


def near_kernel(
    core_ref, xo_hbm, xp_ref, mod_hbm, w_hbm, q_ref, acc_ref, top_ref, mod_ref, w_ref, wq_ref, xo_ref, xn_ref, k_ref, vt_ref, sems
):
    core = core_ref[0]
    own = pltpu.make_async_copy(xo_hbm, xo_ref, sems.at[3])
    mod = pltpu.make_async_copy(mod_hbm, mod_ref, sems.at[4])
    mod.start()
    own.start()
    copies = [
        window_copy(w_hbm, 0, core, wq_ref, sems.at[0]),
        window_copy(w_hbm, 1, core, w_ref.at[:, :WINDOW], sems.at[1]),
        window_copy(w_hbm, 2, core, w_ref.at[:, WINDOW:], sems.at[2]),
    ]
    for copy in copies:
        copy.start()
    mod.wait()
    xn_ref[ROWS:, :] = modulate(xp_ref[...], mod_ref[0:1, :], mod_ref[1:2, :])
    own.wait()
    xn_ref[0:ROWS, :] = modulate(xo_ref[...], mod_ref[0:1, :], mod_ref[1:2, :])
    copies[0].wait()
    queries = jnp.dot(xn_ref[...], wq_ref[...], preferred_element_type=F32)
    q_ref[...] = (queries * QSCALE).astype(BF16)
    copies[1].wait()
    copies[2].wait()
    keys_values(xn_ref[...], w_ref, k_ref, vt_ref)

    def pair(p, carry):
        for h in range(2):
            head = 2 * p + h
            for s, total, top, _ in attend_head(head, core, q_ref, ((k_ref, vt_ref),), None, False):
                width = total.shape[1]
                acc_ref[head, :, s : s + width] = total
                top_ref[head, :, s : s + width] = jnp.broadcast_to(top, (8, width))
        return carry

    lax.fori_loop(0, 4, pair, 0)


def near(core, xo, xp, mod, w):
    return pl.pallas_call(
        near_kernel,
        in_specs=[SMEM, HBM, VMEM, HBM, HBM],
        out_specs=[VMEM] * 5,
        out_shape=[
            jax.ShapeDtypeStruct((LANES, WINDOW), BF16),
            jax.ShapeDtypeStruct((8, AUG, LANES), F32),
            jax.ShapeDtypeStruct((8, 8, LANES), F32),
            jax.ShapeDtypeStruct((6, WIDTH), F32),
            jax.ShapeDtypeStruct((WIDTH, 2 * WINDOW), BF16),
        ],
        scratch_shapes=[
            pltpu.VMEM((WIDTH, WINDOW), BF16),
            pltpu.VMEM((ROWS, WIDTH), BF16),
            pltpu.VMEM((LANES, WIDTH), BF16),
            pltpu.VMEM((LANES, WINDOW), BF16),
            pltpu.VMEM((WINDOW, LANES), F32),
            pltpu.SemaphoreType.DMA((5,)),
        ],
        compiler_params=params(40),
        cost_estimate=pl.CostEstimate(flops=1_000_000, bytes_accessed=100_000, transcendentals=0),
        name="near_tokens",
    )(core, xo, xp, mod, w)


def project_kernel(x_ref, mod_ref, w_ref, k_ref, vt_ref):
    xn = modulate(x_ref[...], mod_ref[0:1, :], mod_ref[1:2, :])
    keys_values(xn, w_ref, k_ref, vt_ref)


def project(x, mod, w):
    return pl.pallas_call(
        project_kernel,
        in_specs=[VMEM] * 3,
        out_specs=[VMEM] * 2,
        out_shape=[jax.ShapeDtypeStruct((ROWS, WINDOW), BF16), jax.ShapeDtypeStruct((WINDOW, ROWS), F32)],
        compiler_params=params(14),
        cost_estimate=pl.CostEstimate(flops=1_000_000, bytes_accessed=100_000, transcendentals=0),
        name="far_keys",
    )(x, mod, w)


def far_kernel(
    core_ref, x_ref, mod_ref, w_ref, k1_ref, vt1_ref, q_ref, acc_ref, top_ref, next_hbm, own_ref, peer_ref, next_ref, k_ref, vt_ref, over_ref, sem
):
    core = core_ref[0]
    ahead = pltpu.make_async_copy(next_hbm, next_ref, sem)
    ahead.start()
    xn = modulate(x_ref[...], mod_ref[0:1, :], mod_ref[1:2, :])
    keys_values(xn, w_ref, k_ref, vt_ref)
    blocks = ((k1_ref, vt1_ref), (k_ref, vt_ref))
    over_ref[...] = jnp.zeros_like(over_ref)

    def attend(known_top):
        def pair(p, carry):
            halves = []
            for h in range(2):
                parts = attend_head(2 * p + h, core, q_ref, blocks, (acc_ref, top_ref), known_top)
                if known_top:
                    for s, total, reference, top in parts:
                        lanes = slice(s, s + total.shape[1])
                        over_ref[0:1, lanes] = jnp.maximum(over_ref[0:1, lanes], top - reference)
                halves.append(
                    jnp.concatenate([t[:HEAD_DIM] / t[HEAD_DIM : HEAD_DIM + 1] for _, t, _, _ in parts], axis=1)
                )
            both = jnp.concatenate(halves, axis=0)
            rows = pl.ds(pl.multiple_of(p * 2 * HEAD_DIM, 16), 2 * HEAD_DIM)
            own_ref[rows, :] = both[:, :ROWS].astype(BF16)
            peer_ref[rows, :] = jnp.concatenate(
                [both[:, ROWS:], jnp.zeros((2 * HEAD_DIM, PADDED - ROWS), F32)], axis=1
            ).astype(BF16)
            return carry

        lax.fori_loop(0, 4, pair, 0)

    attend(True)

    @pl.when(jnp.max(over_ref[...]) > EXCESS)
    def _():
        attend(False)

    ahead.wait()


def far(core, x, mod, w, k1, vt1, q, acc, top, following):
    return pl.pallas_call(
        far_kernel,
        in_specs=[SMEM] + [VMEM] * 8 + [HBM],
        out_specs=[VMEM] * 3,
        out_shape=[
            jax.ShapeDtypeStruct((HALF_COLS, ROWS), BF16),
            jax.ShapeDtypeStruct((HALF_COLS, PADDED), BF16),
            jax.ShapeDtypeStruct((WIDTH, 3 * WIDTH), BF16),
        ],
        scratch_shapes=[
            pltpu.VMEM((ROWS, WINDOW), BF16),
            pltpu.VMEM((WINDOW, ROWS), F32),
            pltpu.VMEM((8, LANES), F32),
            pltpu.SemaphoreType.DMA,
        ],
        compiler_params=params(32),
        cost_estimate=pl.CostEstimate(flops=18_000_000_000, bytes_accessed=10_000_000, transcendentals=6_400_000),
        name="far_tokens",
    )(core, x, mod, w, k1, vt1, q, acc, top, following)


def join_kernel(core_ref, mine_ref, other_ref, x_ref, mod_ref, wo_ref, out_ref, att_ref):
    core = core_ref[0]
    att_ref[pl.ds(pl.multiple_of(core * HALF_COLS, 16), HALF_COLS), :] = mine_ref[...]
    att_ref[pl.ds(pl.multiple_of((1 - core) * HALF_COLS, 16), HALF_COLS), :] = other_ref[:, :ROWS]
    projected = lax.dot_general(att_ref[...], wo_ref[...], TN, preferred_element_type=F32)
    middle = x_ref[...].astype(F32) + mod_ref[2:3, :] * projected
    for d in range(16):
        for i in range(7):
            out_ref[d, i] = middle[28 * d + 4 * i : 28 * d + 4 * i + 4].astype(BF16)


def join(core, mine, other, x, mod, wo):
    return pl.pallas_call(
        join_kernel,
        in_specs=[SMEM] + [VMEM] * 5,
        out_specs=VMEM,
        out_shape=jax.ShapeDtypeStruct((16, 7, 4, WIDTH), BF16),
        scratch_shapes=[pltpu.VMEM((WIDTH, ROWS), BF16)],
        compiler_params=params(14),
        cost_estimate=pl.CostEstimate(flops=1_200_000_000, bytes_accessed=6_000_000, transcendentals=0),
        name="spatial_out",
    )(core, mine, other, x, mod, wo)


def temporal_kernel(mid_ref, mod_ref, w_ref, wo_ref, out_ref, x_ref, q_ref, k_ref, vt_ref, att_ref):
    for f in range(16):
        for i in range(7):
            at = ((i // 2 * 16) + f) * 8 + i % 2 * 4 if i < 6 else 384 + 4 * f
            x_ref[at : at + 4, :] = mid_ref[f, i].astype(F32)
    xn = modulate(x_ref[...], mod_ref[3:4, :], mod_ref[4:5, :])
    packed = jnp.dot(xn, w_ref[...], preferred_element_type=F32)
    q_ref[:, ROWS:] = jnp.zeros((WIDTH, PADDED - ROWS), BF16)
    q_ref[:, :ROWS] = (packed[:, :WIDTH] * QSCALE).T.astype(BF16)
    k_ref[...] = packed[:, WIDTH : 2 * WIDTH].astype(BF16)
    vt_ref[...] = packed[:, 2 * WIDTH :].T

    row = lax.broadcasted_iota(jnp.int32, (256, 1), 0)
    none = jnp.zeros((), BF16)

    def rows_of(g):
        return slice(g * 128, min(g * 128 + 128, ROWS))

    def score(g, p):
        queries = q_ref[128 * p : 128 * p + 256, g * 128 : g * 128 + 128]
        inside = 16 * p
        first = jnp.where((row >= inside) & (row < inside + HEAD_DIM), queries, none)
        second = jnp.where((row >= inside + HEAD_DIM) & (row < inside + 2 * HEAD_DIM), queries, none)
        keys = k_ref[rows_of(g), 128 * p : 128 * p + 256]
        return jnp.dot(keys, jnp.concatenate([first, second], axis=1), preferred_element_type=F32)

    def weigh(g, scores):
        every = 8 if g < 3 else 4
        shape = scores.shape
        key_token = lax.broadcasted_iota(jnp.int32, shape, 0) % every
        same = key_token == lax.broadcasted_iota(jnp.int32, shape, 1) % every
        scores = jnp.where(same, scores, -1e30)
        top = jnp.max(scores, axis=0, keepdims=True)
        return jnp.exp2(scores - top).astype(BF16)

    def value(g, p, weights):
        at = 2 * HEAD_DIM * p
        tail = jnp.where(lax.broadcasted_iota(jnp.int32, (AUG - HEAD_DIM, weights.shape[0]), 0) == 0, 1.0, 0.0)
        first = vt_ref[at : at + HEAD_DIM, rows_of(g)]
        second = vt_ref[at + HEAD_DIM : at + 2 * HEAD_DIM, rows_of(g)]
        values = jnp.concatenate([first, tail, second, tail], axis=0).astype(BF16)
        return jnp.dot(values, weights, preferred_element_type=F32)

    def finish(g, p, total):
        at = 2 * HEAD_DIM * p
        first = total[:HEAD_DIM, :128] / total[HEAD_DIM : HEAD_DIM + 1, :128]
        second = total[AUG : AUG + HEAD_DIM, 128:] / total[AUG + HEAD_DIM : AUG + HEAD_DIM + 1, 128:]
        both = jnp.concatenate([first, second], axis=0).astype(BF16)
        att_ref[at : at + 2 * HEAD_DIM, g * 128 : g * 128 + 128] = both

    order = [(g, p) for g in range(4) for p in range(8)]
    apart = 4
    scores, totals = {}, {}
    for i in range(len(order) + 2 * apart):
        if i < len(order):
            scores[i] = score(*order[i])
        j = i - apart
        if 0 <= j < len(order):
            g, p = order[j]
            totals[j] = value(g, p, weigh(g, scores.pop(j)))
        k = i - 2 * apart
        if 0 <= k < len(order):
            finish(*order[k], totals.pop(k))

    projected = lax.dot_general(att_ref[:, :ROWS], wo_ref[...], TN, preferred_element_type=F32)
    x_ref[...] = x_ref[...] + mod_ref[5:6, :] * projected
    for f in range(16):
        for i in range(7):
            at = ((i // 2 * 16) + f) * 8 + i % 2 * 4 if i < 6 else 384 + 4 * f
            out_ref[f, i] = x_ref[at : at + 4, :].astype(BF16)


def temporal(mid, mod, w, wo):
    return pl.pallas_call(
        temporal_kernel,
        in_specs=[VMEM] * 4,
        out_specs=VMEM,
        out_shape=jax.ShapeDtypeStruct((16, 7, 4, WIDTH), BF16),
        scratch_shapes=[
            pltpu.VMEM((ROWS, WIDTH), F32),
            pltpu.VMEM((WIDTH, PADDED), BF16),
            pltpu.VMEM((ROWS, WIDTH), BF16),
            pltpu.VMEM((WIDTH, ROWS), F32),
            pltpu.VMEM((WIDTH, PADDED), BF16),
        ],
        compiler_params=params(24),
        cost_estimate=pl.CostEstimate(flops=6_000_000_000, bytes_accessed=14_000_000, transcendentals=1_000_000),
        name="temporal_block",
    )(mid, mod, w, wo)


def local(clip, modulation, w_qkv_s, w_out_s, w_qkv_t, w_out_t):
    own = clip[0]
    core = (lax.axis_index("head") % 2).astype(jnp.int32).reshape(1)
    swap_chip = [(0, 2), (1, 3), (2, 0), (3, 1)]
    swap_core = [(0, 1), (1, 0), (2, 3), (3, 2)]
    peer = lax.ppermute(own, "head", swap_core)
    there = lax.ppermute(own, "head", swap_chip)
    q, acc, top, mod, w = near(core, own, peer, modulation, w_qkv_s)
    there, q = lax.optimization_barrier((there, q))
    k1, vt1 = project(there, mod, w)
    there_peer = lax.ppermute(there, "head", swap_core)
    mine, theirs, w_t = far(core, there_peer, mod, w, k1, vt1, q, acc, top, w_qkv_t)
    other = lax.ppermute(theirs, "head", swap_core)
    middle = join(core, mine, other, own, mod, w_out_s)
    block = lax.all_to_all(middle, "tm", split_axis=0, concat_axis=0, tiled=True)
    done = temporal(block, modulation, w_t, w_out_t)
    back = lax.all_to_all(done, "tm", split_axis=0, concat_axis=0, tiled=True)
    return back.reshape(1, ROWS, WIDTH)


def solution(mesh):
    placed = (P(("dp", "tm"), "head", None), P("dp", None), P(), P(), P(), P())
    return jax.shard_map(
        local, mesh=mesh, in_specs=placed, out_specs=P(("dp", "tm"), "head", None), check_vma=False
    )
```

```python
import math

import jax
import jax.numpy as jnp
from jax import lax
from jax.experimental import pallas as pl
from jax.experimental.pallas import tpu as pltpu
from jax.sharding import PartitionSpec as P

HEADS = 16
HEAD_DIM = 72
WIDTH = 1152
ROWS = 448
QUERIES = 896
WINDOW = 640
HALF_COLS = 576
AUG = 80
PADDED = 512
LOOK = 2
QSCALE = math.log2(math.e) / math.sqrt(HEAD_DIM)
NT = (((1,), (1,)), ((), ()))
TN = (((0,), (0,)), ((), ()))
BF16 = jnp.bfloat16
F32 = jnp.float32
VMEM = pl.BlockSpec(memory_space=pltpu.VMEM)
SMEM = pl.BlockSpec(memory_space=pltpu.SMEM)
HBM = pl.BlockSpec(memory_space=pltpu.HBM)
EXCESS = 64.0


def params(mebibytes):
    return pltpu.CompilerParams(vmem_limit_bytes=mebibytes * 1024 * 1024)


def modulate(values, shift_vec, scale_vec):
    values = values.astype(F32)
    average = jnp.mean(values, axis=-1, keepdims=True)
    centred = values - average
    variance = jnp.mean(centred * centred, axis=-1, keepdims=True)
    normed = centred * lax.rsqrt(variance + 1e-06)
    return (normed * (1.0 + scale_vec) + shift_vec).astype(BF16)


def window_copy(w_hbm, third, core, place, sem):
    start = pl.multiple_of(third * WIDTH + core * 512, 128)
    return pltpu.make_async_copy(w_hbm.at[:, pl.ds(start, WINDOW)], place, sem)


def twice(x):
    return x.astype(BF16), jnp.concatenate([x[:, WINDOW - 64 :], x[:, : WINDOW - 64]], axis=1).astype(BF16)


def head_operands(head, core, q_ref, blocks):
    offset = head * HEAD_DIM + core * 64
    turned = (head + core) % 2
    inside = offset + 64 * turned
    start = pl.multiple_of(inside // 128 * 128, 128)
    inside = inside - start
    lane = lax.broadcasted_iota(jnp.int32, (1, 128), 1)
    mine = (lane >= inside) & (lane < inside + HEAD_DIM)
    queries = jnp.where(mine, q_ref[turned, :, pl.ds(start, 128)], jnp.zeros((), BF16))
    keys, values = [], []
    for k_ref, vt_ref in blocks:
        keys.append(k_ref[turned, :, pl.ds(start, 128)])
        first = lax.broadcasted_iota(jnp.int32, (AUG - HEAD_DIM, vt_ref.shape[1]), 0) == 0
        vt = vt_ref[pl.ds(pl.multiple_of(offset, 8), HEAD_DIM), :]
        values.append(jnp.concatenate([vt, jnp.where(first, 1.0, 0.0)], axis=0).astype(BF16))
    return queries, keys, values


def attend_heads(heads, halves, core, q_ref, blocks, old, known_top):
    operands = [head_operands(head, core, q_ref, blocks) for head in heads]
    items = [(i, half) for i in range(len(heads)) for half in halves]

    def score(item):
        i, half = item
        queries, keys, _ = operands[i]
        part = queries[half * ROWS : (half + 1) * ROWS]
        return [lax.dot_general(k, part, NT, preferred_element_type=F32) for k in keys]

    out = []
    ahead = [score(item) for item in items[:LOOK]]
    for n, (i, half) in enumerate(items):
        scores = ahead.pop(0)
        if n + LOOK < len(items):
            ahead.append(score(items[n + LOOK]))
        tops = [jnp.max(part, axis=0, keepdims=True) for part in scores]
        top = tops[0]
        for more in tops[1:]:
            top = jnp.maximum(top, more)
        total = None
        reference = top
        if old is not None:
            acc_ref, top_ref = old
            before = top_ref[half, heads[i], 0:1, :]
            total = acc_ref[half, heads[i]]
            if known_top:
                reference = before
            else:
                reference = jnp.maximum(top, before)
                total = total * jnp.exp2(before - reference)
        for value, part in zip(operands[i][2], scores):
            term = jnp.dot(value, jnp.exp2(part - reference).astype(BF16), preferred_element_type=F32)
            total = term if total is None else total + term
        out.append((total, reference, top))
    return out


def keys_values(xn, w_ref, k_ref, vt_ref):
    packed = jnp.dot(xn, w_ref[...], preferred_element_type=F32)
    k_ref[0], k_ref[1] = twice(packed[:, :WINDOW])
    vt_ref[...] = packed[:, WINDOW:].T


def near_kernel(
    core_ref, xo_hbm, xp_ref, mod_hbm, w_hbm, next_hbm, q_ref, acc_ref, top_ref, mod_ref, w_ref, next_ref, wq_ref, xo_ref, xn_ref, k_ref, vt_ref, sems
):
    core = core_ref[0]
    own = pltpu.make_async_copy(xo_hbm, xo_ref, sems.at[3])
    mod = pltpu.make_async_copy(mod_hbm, mod_ref, sems.at[4])
    mod.start()
    own.start()
    copies = [
        window_copy(w_hbm, 0, core, wq_ref, sems.at[0]),
        window_copy(w_hbm, 1, core, w_ref.at[:, :WINDOW], sems.at[1]),
        window_copy(w_hbm, 2, core, w_ref.at[:, WINDOW:], sems.at[2]),
    ]
    for copy in copies:
        copy.start()
    following = pltpu.make_async_copy(next_hbm, next_ref, sems.at[5])
    following.start()
    mod.wait()
    xn_ref[ROWS:, :] = modulate(xp_ref[...], mod_ref[0:1, :], mod_ref[1:2, :])
    own.wait()
    xn_ref[0:ROWS, :] = modulate(xo_ref[...], mod_ref[0:1, :], mod_ref[1:2, :])
    copies[0].wait()
    queries = jnp.dot(xn_ref[...], wq_ref[...], preferred_element_type=F32)
    q_ref[0], q_ref[1] = twice(queries * QSCALE)
    copies[1].wait()
    copies[2].wait()
    keys_values(xn_ref[...], w_ref, k_ref, vt_ref)

    results = attend_heads(range(8), (0, 1), core, q_ref, ((k_ref, vt_ref),), None, False)
    for n, (total, top, _) in enumerate(results):
        acc_ref[n % 2, n // 2] = total
        top_ref[n % 2, n // 2] = jnp.broadcast_to(top, (8, ROWS))
    following.wait()


def near(core, xo, xp, mod, w, following):
    return pl.pallas_call(
        near_kernel,
        in_specs=[SMEM, HBM, VMEM, HBM, HBM, HBM],
        out_specs=[VMEM] * 6,
        out_shape=[
            jax.ShapeDtypeStruct((2, QUERIES, WINDOW), BF16),
            jax.ShapeDtypeStruct((2, 8, AUG, ROWS), F32),
            jax.ShapeDtypeStruct((2, 8, 8, ROWS), F32),
            jax.ShapeDtypeStruct((6, WIDTH), F32),
            jax.ShapeDtypeStruct((WIDTH, 2 * WINDOW), BF16),
            jax.ShapeDtypeStruct((WIDTH, 3 * WIDTH), BF16),
        ],
        scratch_shapes=[
            pltpu.VMEM((WIDTH, WINDOW), BF16),
            pltpu.VMEM((ROWS, WIDTH), BF16),
            pltpu.VMEM((QUERIES, WIDTH), BF16),
            pltpu.VMEM((2, QUERIES, WINDOW), BF16),
            pltpu.VMEM((WINDOW, QUERIES), F32),
            pltpu.SemaphoreType.DMA((6,)),
        ],
        compiler_params=params(36),
        cost_estimate=pl.CostEstimate(flops=1_000_000, bytes_accessed=100_000, transcendentals=0),
        name="near_tokens",
    )(core, xo, xp, mod, w, following)


def project_kernel(x_ref, mod_ref, w_ref, k_ref, vt_ref):
    xn = modulate(x_ref[...], mod_ref[0:1, :], mod_ref[1:2, :])
    keys_values(xn, w_ref, k_ref, vt_ref)


def project(x, mod, w):
    return pl.pallas_call(
        project_kernel,
        in_specs=[VMEM] * 3,
        out_specs=[VMEM] * 2,
        out_shape=[jax.ShapeDtypeStruct((2, ROWS, WINDOW), BF16), jax.ShapeDtypeStruct((WINDOW, ROWS), F32)],
        compiler_params=params(14),
        cost_estimate=pl.CostEstimate(flops=1_000_000, bytes_accessed=100_000, transcendentals=0),
        name="far_keys",
    )(x, mod, w)


def attend_far(half, core, q_ref, blocks, acc_ref, top_ref, out_ref, over_ref):
    def attend(first, count, known_top):
        heads = [first + i for i in range(count)]
        done = []
        for total, reference, top in attend_heads(heads, (half,), core, q_ref, blocks, (acc_ref, top_ref), known_top):
            if known_top:
                over_ref[0:1, :] = jnp.maximum(over_ref[0:1, :], top - reference)
            done.append(total[:HEAD_DIM] / total[HEAD_DIM : HEAD_DIM + 1])
        for i in range(0, count, 2):
            rows = pl.ds(pl.multiple_of((first + i) * HEAD_DIM, 16), 2 * HEAD_DIM)
            out_ref[rows, :ROWS] = jnp.concatenate(done[i : i + 2], axis=0).astype(BF16)

    over_ref[...] = jnp.zeros_like(over_ref)
    attend(0, 8, True)

    @pl.when(jnp.max(over_ref[...]) > EXCESS)
    def _():
        def pair(p, carry):
            attend(2 * p, 2, False)
            return carry

        lax.fori_loop(0, 4, pair, 0)


def far_peer_kernel(
    core_ref, x_ref, mod_ref, w_ref, k1_ref, vt1_ref, q_ref, acc_ref, top_ref, out_ref, k_ref, vt_ref, over_ref
):
    xn = modulate(x_ref[...], mod_ref[0:1, :], mod_ref[1:2, :])
    keys_values(xn, w_ref, k_ref, vt_ref)
    out_ref[:, ROWS:] = jnp.zeros((HALF_COLS, PADDED - ROWS), BF16)
    blocks = ((k1_ref, vt1_ref), (k_ref, vt_ref))
    attend_far(1, core_ref[0], q_ref, blocks, acc_ref, top_ref, out_ref, over_ref)


def far_peer(core, x, mod, w, k1, vt1, q, acc, top):
    return pl.pallas_call(
        far_peer_kernel,
        in_specs=[SMEM] + [VMEM] * 8,
        out_specs=[VMEM] * 3,
        out_shape=[
            jax.ShapeDtypeStruct((HALF_COLS, PADDED), BF16),
            jax.ShapeDtypeStruct((2, ROWS, WINDOW), BF16),
            jax.ShapeDtypeStruct((WINDOW, ROWS), F32),
        ],
        scratch_shapes=[pltpu.VMEM((8, ROWS), F32)],
        compiler_params=params(28),
        cost_estimate=pl.CostEstimate(flops=10_000_000_000, bytes_accessed=10_000_000, transcendentals=3_200_000),
        name="far_peer_queries",
    )(core, x, mod, w, k1, vt1, q, acc, top)


def far_own_kernel(core_ref, k1_ref, vt1_ref, k2_ref, vt2_ref, q_ref, acc_ref, top_ref, out_ref, over_ref):
    blocks = ((k1_ref, vt1_ref), (k2_ref, vt2_ref))
    attend_far(0, core_ref[0], q_ref, blocks, acc_ref, top_ref, out_ref, over_ref)


def far_own(core, k1, vt1, k2, vt2, q, acc, top):
    return pl.pallas_call(
        far_own_kernel,
        in_specs=[SMEM] + [VMEM] * 7,
        out_specs=VMEM,
        out_shape=jax.ShapeDtypeStruct((HALF_COLS, ROWS), BF16),
        scratch_shapes=[pltpu.VMEM((8, ROWS), F32)],
        compiler_params=params(24),
        cost_estimate=pl.CostEstimate(flops=8_000_000_000, bytes_accessed=5_000_000, transcendentals=3_200_000),
        name="far_own_queries",
    )(core, k1, vt1, k2, vt2, q, acc, top)


def join_kernel(core_ref, mine_ref, other_ref, x_ref, mod_ref, wo_ref, out_ref, att_ref):
    core = core_ref[0]
    att_ref[pl.ds(pl.multiple_of(core * HALF_COLS, 16), HALF_COLS), :] = mine_ref[...]
    att_ref[pl.ds(pl.multiple_of((1 - core) * HALF_COLS, 16), HALF_COLS), :] = other_ref[:, :ROWS]
    projected = lax.dot_general(att_ref[...], wo_ref[...], TN, preferred_element_type=F32)
    middle = x_ref[...].astype(F32) + mod_ref[2:3, :] * projected
    for d in range(16):
        for i in range(7):
            out_ref[d, i] = middle[28 * d + 4 * i : 28 * d + 4 * i + 4].astype(BF16)


def join(core, mine, other, x, mod, wo):
    return pl.pallas_call(
        join_kernel,
        in_specs=[SMEM] + [VMEM] * 5,
        out_specs=VMEM,
        out_shape=jax.ShapeDtypeStruct((16, 7, 4, WIDTH), BF16),
        scratch_shapes=[pltpu.VMEM((WIDTH, ROWS), BF16)],
        compiler_params=params(14),
        cost_estimate=pl.CostEstimate(flops=1_200_000_000, bytes_accessed=6_000_000, transcendentals=0),
        name="spatial_out",
    )(core, mine, other, x, mod, wo)


def temporal_kernel(mid_ref, mod_ref, w_ref, wo_ref, out_ref, x_ref, q_ref, k_ref, vt_ref, att_ref):
    for f in range(16):
        for i in range(7):
            at = ((i // 2 * 16) + f) * 8 + i % 2 * 4 if i < 6 else 384 + 4 * f
            x_ref[at : at + 4, :] = mid_ref[f, i].astype(F32)
    xn = modulate(x_ref[...], mod_ref[3:4, :], mod_ref[4:5, :])
    packed = jnp.dot(xn, w_ref[...], preferred_element_type=F32)
    q_ref[:, ROWS:] = jnp.zeros((WIDTH, PADDED - ROWS), BF16)
    q_ref[:, :ROWS] = (packed[:, :WIDTH] * QSCALE).T.astype(BF16)
    k_ref[...] = packed[:, WIDTH : 2 * WIDTH].astype(BF16)
    vt_ref[...] = packed[:, 2 * WIDTH :].T

    row = lax.broadcasted_iota(jnp.int32, (256, 1), 0)
    none = jnp.zeros((), BF16)

    def rows_of(g):
        return slice(g * 128, min(g * 128 + 128, ROWS))

    def score(g, p):
        queries = q_ref[128 * p : 128 * p + 256, g * 128 : g * 128 + 128]
        inside = 16 * p
        first = jnp.where((row >= inside) & (row < inside + HEAD_DIM), queries, none)
        second = jnp.where((row >= inside + HEAD_DIM) & (row < inside + 2 * HEAD_DIM), queries, none)
        keys = k_ref[rows_of(g), 128 * p : 128 * p + 256]
        return jnp.dot(keys, jnp.concatenate([first, second], axis=1), preferred_element_type=F32)

    def weigh(g, scores):
        every = 8 if g < 3 else 4
        shape = scores.shape
        key_token = lax.broadcasted_iota(jnp.int32, shape, 0) % every
        same = key_token == lax.broadcasted_iota(jnp.int32, shape, 1) % every
        scores = jnp.where(same, scores, -1e30)
        top = jnp.max(scores, axis=0, keepdims=True)
        return jnp.exp2(scores - top).astype(BF16)

    def value(g, p, weights):
        at = 2 * HEAD_DIM * p
        tail = jnp.where(lax.broadcasted_iota(jnp.int32, (AUG - HEAD_DIM, weights.shape[0]), 0) == 0, 1.0, 0.0)
        first = vt_ref[at : at + HEAD_DIM, rows_of(g)]
        second = vt_ref[at + HEAD_DIM : at + 2 * HEAD_DIM, rows_of(g)]
        values = jnp.concatenate([first, tail, second, tail], axis=0).astype(BF16)
        return jnp.dot(values, weights, preferred_element_type=F32)

    def finish(g, p, total):
        at = 2 * HEAD_DIM * p
        first = total[:HEAD_DIM, :128] / total[HEAD_DIM : HEAD_DIM + 1, :128]
        second = total[AUG : AUG + HEAD_DIM, 128:] / total[AUG + HEAD_DIM : AUG + HEAD_DIM + 1, 128:]
        both = jnp.concatenate([first, second], axis=0).astype(BF16)
        att_ref[at : at + 2 * HEAD_DIM, g * 128 : g * 128 + 128] = both

    order = [(g, p) for g in range(4) for p in range(8)]
    apart = 4
    scores, totals = {}, {}
    for i in range(len(order) + 2 * apart):
        if i < len(order):
            scores[i] = score(*order[i])
        j = i - apart
        if 0 <= j < len(order):
            g, p = order[j]
            totals[j] = value(g, p, weigh(g, scores.pop(j)))
        k = i - 2 * apart
        if 0 <= k < len(order):
            finish(*order[k], totals.pop(k))

    projected = lax.dot_general(att_ref[:, :ROWS], wo_ref[...], TN, preferred_element_type=F32)
    x_ref[...] = x_ref[...] + mod_ref[5:6, :] * projected
    for f in range(16):
        for i in range(7):
            at = ((i // 2 * 16) + f) * 8 + i % 2 * 4 if i < 6 else 384 + 4 * f
            out_ref[f, i] = x_ref[at : at + 4, :].astype(BF16)


def temporal(mid, mod, w, wo):
    return pl.pallas_call(
        temporal_kernel,
        in_specs=[VMEM] * 4,
        out_specs=VMEM,
        out_shape=jax.ShapeDtypeStruct((16, 7, 4, WIDTH), BF16),
        scratch_shapes=[
            pltpu.VMEM((ROWS, WIDTH), F32),
            pltpu.VMEM((WIDTH, PADDED), BF16),
            pltpu.VMEM((ROWS, WIDTH), BF16),
            pltpu.VMEM((WIDTH, ROWS), F32),
            pltpu.VMEM((WIDTH, PADDED), BF16),
        ],
        compiler_params=params(24),
        cost_estimate=pl.CostEstimate(flops=6_000_000_000, bytes_accessed=14_000_000, transcendentals=1_000_000),
        name="temporal_block",
    )(mid, mod, w, wo)


def local(clip, modulation, w_qkv_s, w_out_s, w_qkv_t, w_out_t):
    own = clip[0]
    core = (lax.axis_index("head") % 2).astype(jnp.int32).reshape(1)
    swap_chip = [(0, 2), (1, 3), (2, 0), (3, 1)]
    swap_core = [(0, 1), (1, 0), (2, 3), (3, 2)]
    peer = lax.ppermute(own, "head", swap_core)
    there = lax.ppermute(own, "head", swap_chip)
    q, acc, top, mod, w, w_t = near(core, own, peer, modulation, w_qkv_s, w_qkv_t)
    there, q = lax.optimization_barrier((there, q))
    k1, vt1 = project(there, mod, w)
    there_peer = lax.ppermute(there, "head", swap_core)
    theirs, k2, vt2 = far_peer(core, there_peer, mod, w, k1, vt1, q, acc, top)
    other = lax.ppermute(theirs, "head", swap_core)
    mine = far_own(core, k1, vt1, k2, vt2, q, acc, top)
    middle = join(core, mine, other, own, mod, w_out_s)
    block = lax.all_to_all(middle, "tm", split_axis=0, concat_axis=0, tiled=True)
    done = temporal(block, modulation, w_t, w_out_t)
    back = lax.all_to_all(done, "tm", split_axis=0, concat_axis=0, tiled=True)
    return back.reshape(1, ROWS, WIDTH)


def solution(mesh):
    placed = (P(("dp", "tm"), "head", None), P("dp", None), P(), P(), P(), P())
    return jax.shard_map(
        local, mesh=mesh, in_specs=placed, out_specs=P(("dp", "tm"), "head", None), check_vma=False
    )
```

```python
import math

import jax
import jax.numpy as jnp
from jax import lax
from jax.experimental import pallas as pl
from jax.experimental.pallas import tpu as pltpu
from jax.sharding import PartitionSpec as P

HEADS = 16
HEAD_DIM = 72
WIDTH = 1152
ROWS = 448
QUERIES = 896
WINDOW = 640
HALF_COLS = 576
AUG = 80
PADDED = 512
LOOK = 2
QSCALE = math.log2(math.e) / math.sqrt(HEAD_DIM)
NT = (((1,), (1,)), ((), ()))
TN = (((0,), (0,)), ((), ()))
BF16 = jnp.bfloat16
F32 = jnp.float32
VMEM = pl.BlockSpec(memory_space=pltpu.VMEM)
SMEM = pl.BlockSpec(memory_space=pltpu.SMEM)
HBM = pl.BlockSpec(memory_space=pltpu.HBM)
EXCESS = 64.0


def params(mebibytes):
    return pltpu.CompilerParams(vmem_limit_bytes=mebibytes * 1024 * 1024)


def modulate(values, shift_vec, scale_vec):
    values = values.astype(F32)
    average = jnp.mean(values, axis=-1, keepdims=True)
    centred = values - average
    variance = jnp.mean(centred * centred, axis=-1, keepdims=True)
    normed = centred * lax.rsqrt(variance + 1e-06)
    return (normed * (1.0 + scale_vec) + shift_vec).astype(BF16)


def window_copy(w_hbm, third, core, place, sem):
    start = pl.multiple_of(third * WIDTH + core * 512, 128)
    return pltpu.make_async_copy(w_hbm.at[:, pl.ds(start, WINDOW)], place, sem)


def twice(x):
    return x.astype(BF16), jnp.concatenate([x[:, WINDOW - 64 :], x[:, : WINDOW - 64]], axis=1).astype(BF16)


def head_operands(head, core, q_ref, blocks):
    offset = head * HEAD_DIM + core * 64
    turned = (head + core) % 2
    inside = offset + 64 * turned
    start = pl.multiple_of(inside // 128 * 128, 128)
    inside = inside - start
    lane = lax.broadcasted_iota(jnp.int32, (1, 128), 1)
    mine = (lane >= inside) & (lane < inside + HEAD_DIM)
    queries = jnp.where(mine, q_ref[turned, :, pl.ds(start, 128)], jnp.zeros((), BF16))
    keys, values = [], []
    for k_ref, vt_ref in blocks:
        keys.append(k_ref[turned, :, pl.ds(start, 128)])
        first = lax.broadcasted_iota(jnp.int32, (AUG - HEAD_DIM, vt_ref.shape[1]), 0) == 0
        vt = vt_ref[pl.ds(pl.multiple_of(offset, 8), HEAD_DIM), :]
        values.append(jnp.concatenate([vt, jnp.where(first, 1.0, 0.0)], axis=0).astype(BF16))
    return queries, keys, values


def attend_heads(heads, halves, core, q_ref, blocks, old, known_top):
    operands = [head_operands(head, core, q_ref, blocks) for head in heads]
    items = [(i, half) for i in range(len(heads)) for half in halves]

    def score(item):
        i, half = item
        queries, keys, _ = operands[i]
        part = queries[half * ROWS : (half + 1) * ROWS]
        return [lax.dot_general(k, part, NT, preferred_element_type=F32) for k in keys]

    out = []
    ahead = [score(item) for item in items[:LOOK]]
    for n, (i, half) in enumerate(items):
        scores = ahead.pop(0)
        if n + LOOK < len(items):
            ahead.append(score(items[n + LOOK]))
        tops = [jnp.max(part, axis=0, keepdims=True) for part in scores]
        top = tops[0]
        for more in tops[1:]:
            top = jnp.maximum(top, more)
        total = None
        reference = top
        if old is not None:
            acc_ref, top_ref = old
            before = top_ref[half, heads[i], 0:1, :]
            total = acc_ref[half, heads[i]]
            if known_top:
                reference = before
            else:
                reference = jnp.maximum(top, before)
                total = total * jnp.exp2(before - reference)
        for value, part in zip(operands[i][2], scores):
            term = jnp.dot(value, jnp.exp2(part - reference).astype(BF16), preferred_element_type=F32)
            total = term if total is None else total + term
        out.append((total, reference, top))
    return out


def keys_values(xn, w_ref, k_ref, vt_ref):
    packed = jnp.dot(xn, w_ref[...], preferred_element_type=F32)
    k_ref[0], k_ref[1] = twice(packed[:, :WINDOW])
    vt_ref[...] = packed[:, WINDOW:].T


def near_kernel(
    core_ref, xo_hbm, xp_ref, mod_hbm, w_hbm, next_hbm, q_ref, acc_ref, top_ref, mod_ref, w_ref, next_ref, wq_ref, xo_ref, xn_ref, k_ref, vt_ref, sems
):
    core = core_ref[0]
    own = pltpu.make_async_copy(xo_hbm, xo_ref, sems.at[3])
    mod = pltpu.make_async_copy(mod_hbm, mod_ref, sems.at[4])
    mod.start()
    own.start()
    copies = [
        window_copy(w_hbm, 0, core, wq_ref, sems.at[0]),
        window_copy(w_hbm, 1, core, w_ref.at[:, :WINDOW], sems.at[1]),
        window_copy(w_hbm, 2, core, w_ref.at[:, WINDOW:], sems.at[2]),
    ]
    for copy in copies:
        copy.start()
    following = pltpu.make_async_copy(next_hbm, next_ref, sems.at[5])
    following.start()
    mod.wait()
    xn_ref[ROWS:, :] = modulate(xp_ref[...], mod_ref[0:1, :], mod_ref[1:2, :])
    own.wait()
    xn_ref[0:ROWS, :] = modulate(xo_ref[...], mod_ref[0:1, :], mod_ref[1:2, :])
    copies[0].wait()
    queries = jnp.dot(xn_ref[...], wq_ref[...], preferred_element_type=F32)
    q_ref[0], q_ref[1] = twice(queries * QSCALE)
    copies[1].wait()
    copies[2].wait()
    keys_values(xn_ref[...], w_ref, k_ref, vt_ref)


    def some(p, carry):
        heads = [2 * p + i for i in range(2)]
        results = attend_heads(heads, (0, 1), core, q_ref, ((k_ref, vt_ref),), None, False)
        for n, (total, top, _) in enumerate(results):
            acc_ref[n % 2, heads[n // 2]] = total
            top_ref[n % 2, heads[n // 2]] = jnp.broadcast_to(top, (8, ROWS))
        return carry

    lax.fori_loop(0, 8 // 2, some, 0)
    following.wait()


def near(core, xo, xp, mod, w, following):
    return pl.pallas_call(
        near_kernel,
        in_specs=[SMEM, HBM, VMEM, HBM, HBM, HBM],
        out_specs=[VMEM] * 6,
        out_shape=[
            jax.ShapeDtypeStruct((2, QUERIES, WINDOW), BF16),
            jax.ShapeDtypeStruct((2, 8, AUG, ROWS), F32),
            jax.ShapeDtypeStruct((2, 8, 8, ROWS), F32),
            jax.ShapeDtypeStruct((6, WIDTH), F32),
            jax.ShapeDtypeStruct((WIDTH, 2 * WINDOW), BF16),
            jax.ShapeDtypeStruct((WIDTH, 3 * WIDTH), BF16),
        ],
        scratch_shapes=[
            pltpu.VMEM((WIDTH, WINDOW), BF16),
            pltpu.VMEM((ROWS, WIDTH), BF16),
            pltpu.VMEM((QUERIES, WIDTH), BF16),
            pltpu.VMEM((2, QUERIES, WINDOW), BF16),
            pltpu.VMEM((WINDOW, QUERIES), F32),
            pltpu.SemaphoreType.DMA((6,)),
        ],
        compiler_params=params(36),
        cost_estimate=pl.CostEstimate(flops=1_000_000, bytes_accessed=100_000, transcendentals=0),
        name="near_tokens",
    )(core, xo, xp, mod, w, following)


def project_kernel(x_ref, mod_ref, w_ref, k_ref, vt_ref):
    xn = modulate(x_ref[...], mod_ref[0:1, :], mod_ref[1:2, :])
    keys_values(xn, w_ref, k_ref, vt_ref)


def project(x, mod, w):
    return pl.pallas_call(
        project_kernel,
        in_specs=[VMEM] * 3,
        out_specs=[VMEM] * 2,
        out_shape=[jax.ShapeDtypeStruct((2, ROWS, WINDOW), BF16), jax.ShapeDtypeStruct((WINDOW, ROWS), F32)],
        compiler_params=params(14),
        cost_estimate=pl.CostEstimate(flops=1_000_000, bytes_accessed=100_000, transcendentals=0),
        name="far_keys",
    )(x, mod, w)


def attend_far(half, core, q_ref, blocks, acc_ref, top_ref, out_ref, over_ref):
    def attend(first, count, known_top):
        heads = [first + i for i in range(count)]
        done = []
        for total, reference, top in attend_heads(heads, (half,), core, q_ref, blocks, (acc_ref, top_ref), known_top):
            if known_top:
                over_ref[0:1, :] = jnp.maximum(over_ref[0:1, :], top - reference)
            done.append(total[:HEAD_DIM] / total[HEAD_DIM : HEAD_DIM + 1])
        for i in range(0, count, 2):
            rows = pl.ds(pl.multiple_of((first + i) * HEAD_DIM, 16), 2 * HEAD_DIM)
            out_ref[rows, :ROWS] = jnp.concatenate(done[i : i + 2], axis=0).astype(BF16)

    over_ref[...] = jnp.zeros_like(over_ref)
    attend(0, 8, True)

    @pl.when(jnp.max(over_ref[...]) > EXCESS)
    def _():
        def pair(p, carry):
            attend(2 * p, 2, False)
            return carry

        lax.fori_loop(0, 4, pair, 0)


def far_peer_kernel(
    core_ref, x_ref, mod_ref, w_ref, k1_ref, vt1_ref, q_ref, acc_ref, top_ref, out_ref, k_ref, vt_ref, over_ref
):
    xn = modulate(x_ref[...], mod_ref[0:1, :], mod_ref[1:2, :])
    keys_values(xn, w_ref, k_ref, vt_ref)
    out_ref[:, ROWS:] = jnp.zeros((HALF_COLS, PADDED - ROWS), BF16)
    blocks = ((k1_ref, vt1_ref), (k_ref, vt_ref))
    attend_far(1, core_ref[0], q_ref, blocks, acc_ref, top_ref, out_ref, over_ref)


def far_peer(core, x, mod, w, k1, vt1, q, acc, top):
    return pl.pallas_call(
        far_peer_kernel,
        in_specs=[SMEM] + [VMEM] * 8,
        out_specs=[VMEM] * 3,
        out_shape=[
            jax.ShapeDtypeStruct((HALF_COLS, PADDED), BF16),
            jax.ShapeDtypeStruct((2, ROWS, WINDOW), BF16),
            jax.ShapeDtypeStruct((WINDOW, ROWS), F32),
        ],
        scratch_shapes=[pltpu.VMEM((8, ROWS), F32)],
        compiler_params=params(28),
        cost_estimate=pl.CostEstimate(flops=10_000_000_000, bytes_accessed=10_000_000, transcendentals=3_200_000),
        name="far_peer_queries",
    )(core, x, mod, w, k1, vt1, q, acc, top)


def far_own_kernel(core_ref, k1_ref, vt1_ref, k2_ref, vt2_ref, q_ref, acc_ref, top_ref, out_ref, over_ref):
    blocks = ((k1_ref, vt1_ref), (k2_ref, vt2_ref))
    attend_far(0, core_ref[0], q_ref, blocks, acc_ref, top_ref, out_ref, over_ref)


def far_own(core, k1, vt1, k2, vt2, q, acc, top):
    return pl.pallas_call(
        far_own_kernel,
        in_specs=[SMEM] + [VMEM] * 7,
        out_specs=VMEM,
        out_shape=jax.ShapeDtypeStruct((HALF_COLS, ROWS), BF16),
        scratch_shapes=[pltpu.VMEM((8, ROWS), F32)],
        compiler_params=params(24),
        cost_estimate=pl.CostEstimate(flops=8_000_000_000, bytes_accessed=5_000_000, transcendentals=3_200_000),
        name="far_own_queries",
    )(core, k1, vt1, k2, vt2, q, acc, top)


def join_kernel(core_ref, mine_ref, other_ref, x_ref, mod_ref, wo_ref, out_ref, att_ref):
    core = core_ref[0]
    att_ref[pl.ds(pl.multiple_of(core * HALF_COLS, 16), HALF_COLS), :] = mine_ref[...]
    att_ref[pl.ds(pl.multiple_of((1 - core) * HALF_COLS, 16), HALF_COLS), :] = other_ref[:, :ROWS]
    projected = lax.dot_general(att_ref[...], wo_ref[...], TN, preferred_element_type=F32)
    middle = x_ref[...].astype(F32) + mod_ref[2:3, :] * projected
    for d in range(16):
        for i in range(7):
            out_ref[d, i] = middle[28 * d + 4 * i : 28 * d + 4 * i + 4].astype(BF16)


def join(core, mine, other, x, mod, wo):
    return pl.pallas_call(
        join_kernel,
        in_specs=[SMEM] + [VMEM] * 5,
        out_specs=VMEM,
        out_shape=jax.ShapeDtypeStruct((16, 7, 4, WIDTH), BF16),
        scratch_shapes=[pltpu.VMEM((WIDTH, ROWS), BF16)],
        compiler_params=params(14),
        cost_estimate=pl.CostEstimate(flops=1_200_000_000, bytes_accessed=6_000_000, transcendentals=0),
        name="spatial_out",
    )(core, mine, other, x, mod, wo)


def temporal_kernel(mid_ref, mod_ref, w_ref, wo_ref, out_ref, x_ref, q_ref, k_ref, vt_ref, att_ref):
    for f in range(16):
        for i in range(7):
            at = ((i // 2 * 16) + f) * 8 + i % 2 * 4 if i < 6 else 384 + 4 * f
            x_ref[at : at + 4, :] = mid_ref[f, i].astype(F32)
    xn = modulate(x_ref[...], mod_ref[3:4, :], mod_ref[4:5, :])
    packed = jnp.dot(xn, w_ref[...], preferred_element_type=F32)
    q_ref[:, ROWS:] = jnp.zeros((WIDTH, PADDED - ROWS), BF16)
    q_ref[:, :ROWS] = (packed[:, :WIDTH] * QSCALE).T.astype(BF16)
    k_ref[...] = packed[:, WIDTH : 2 * WIDTH].astype(BF16)
    vt_ref[...] = packed[:, 2 * WIDTH :].T

    row = lax.broadcasted_iota(jnp.int32, (256, 1), 0)
    none = jnp.zeros((), BF16)

    def rows_of(g):
        return slice(g * 128, min(g * 128 + 128, ROWS))

    def score(g, p):
        queries = q_ref[128 * p : 128 * p + 256, g * 128 : g * 128 + 128]
        inside = 16 * p
        first = jnp.where((row >= inside) & (row < inside + HEAD_DIM), queries, none)
        second = jnp.where((row >= inside + HEAD_DIM) & (row < inside + 2 * HEAD_DIM), queries, none)
        keys = k_ref[rows_of(g), 128 * p : 128 * p + 256]
        return jnp.dot(keys, jnp.concatenate([first, second], axis=1), preferred_element_type=F32)

    def weigh(g, scores):
        every = 8 if g < 3 else 4
        shape = scores.shape
        key_token = lax.broadcasted_iota(jnp.int32, shape, 0) % every
        same = key_token == lax.broadcasted_iota(jnp.int32, shape, 1) % every
        scores = jnp.where(same, scores, -1e30)
        top = jnp.max(scores, axis=0, keepdims=True)
        return jnp.exp2(scores - top).astype(BF16)

    def value(g, p, weights):
        at = 2 * HEAD_DIM * p
        tail = jnp.where(lax.broadcasted_iota(jnp.int32, (AUG - HEAD_DIM, weights.shape[0]), 0) == 0, 1.0, 0.0)
        first = vt_ref[at : at + HEAD_DIM, rows_of(g)]
        second = vt_ref[at + HEAD_DIM : at + 2 * HEAD_DIM, rows_of(g)]
        values = jnp.concatenate([first, tail, second, tail], axis=0).astype(BF16)
        return jnp.dot(values, weights, preferred_element_type=F32)

    def finish(g, p, total):
        at = 2 * HEAD_DIM * p
        first = total[:HEAD_DIM, :128] / total[HEAD_DIM : HEAD_DIM + 1, :128]
        second = total[AUG : AUG + HEAD_DIM, 128:] / total[AUG + HEAD_DIM : AUG + HEAD_DIM + 1, 128:]
        both = jnp.concatenate([first, second], axis=0).astype(BF16)
        att_ref[at : at + 2 * HEAD_DIM, g * 128 : g * 128 + 128] = both

    order = [(g, p) for g in range(4) for p in range(8)]
    apart = 4
    scores, totals = {}, {}
    for i in range(len(order) + 2 * apart):
        if i < len(order):
            scores[i] = score(*order[i])
        j = i - apart
        if 0 <= j < len(order):
            g, p = order[j]
            totals[j] = value(g, p, weigh(g, scores.pop(j)))
        k = i - 2 * apart
        if 0 <= k < len(order):
            finish(*order[k], totals.pop(k))

    projected = lax.dot_general(att_ref[:, :ROWS], wo_ref[...], TN, preferred_element_type=F32)
    x_ref[...] = x_ref[...] + mod_ref[5:6, :] * projected
    for f in range(16):
        for i in range(7):
            at = ((i // 2 * 16) + f) * 8 + i % 2 * 4 if i < 6 else 384 + 4 * f
            out_ref[f, i] = x_ref[at : at + 4, :].astype(BF16)


def temporal(mid, mod, w, wo):
    return pl.pallas_call(
        temporal_kernel,
        in_specs=[VMEM] * 4,
        out_specs=VMEM,
        out_shape=jax.ShapeDtypeStruct((16, 7, 4, WIDTH), BF16),
        scratch_shapes=[
            pltpu.VMEM((ROWS, WIDTH), F32),
            pltpu.VMEM((WIDTH, PADDED), BF16),
            pltpu.VMEM((ROWS, WIDTH), BF16),
            pltpu.VMEM((WIDTH, ROWS), F32),
            pltpu.VMEM((WIDTH, PADDED), BF16),
        ],
        compiler_params=params(24),
        cost_estimate=pl.CostEstimate(flops=6_000_000_000, bytes_accessed=14_000_000, transcendentals=1_000_000),
        name="temporal_block",
    )(mid, mod, w, wo)


def local(clip, modulation, w_qkv_s, w_out_s, w_qkv_t, w_out_t):
    own = clip[0]
    core = (lax.axis_index("head") % 2).astype(jnp.int32).reshape(1)
    swap_chip = [(0, 2), (1, 3), (2, 0), (3, 1)]
    swap_core = [(0, 1), (1, 0), (2, 3), (3, 2)]
    peer = lax.ppermute(own, "head", swap_core)
    there = lax.ppermute(own, "head", swap_chip)
    q, acc, top, mod, w, w_t = near(core, own, peer, modulation, w_qkv_s, w_qkv_t)
    there, q = lax.optimization_barrier((there, q))
    k1, vt1 = project(there, mod, w)
    there_peer = lax.ppermute(there, "head", swap_core)
    theirs, k2, vt2 = far_peer(core, there_peer, mod, w, k1, vt1, q, acc, top)
    other = lax.ppermute(theirs, "head", swap_core)
    mine = far_own(core, k1, vt1, k2, vt2, q, acc, top)
    middle = join(core, mine, other, own, mod, w_out_s)
    block = lax.all_to_all(middle, "tm", split_axis=0, concat_axis=0, tiled=True)
    done = temporal(block, modulation, w_t, w_out_t)
    back = lax.all_to_all(done, "tm", split_axis=0, concat_axis=0, tiled=True)
    return back.reshape(1, ROWS, WIDTH)


def solution(mesh):
    placed = (P(("dp", "tm"), "head", None), P("dp", None), P(), P(), P(), P())
    return jax.shard_map(
        local, mesh=mesh, in_specs=placed, out_specs=P(("dp", "tm"), "head", None), check_vma=False
    )
```

```python
import math

import jax
import jax.numpy as jnp
from jax import lax
from jax.experimental import pallas as pl
from jax.experimental.pallas import tpu as pltpu
from jax.sharding import PartitionSpec as P

HEADS = 16
HEAD_DIM = 72
WIDTH = 1152
ROWS = 448
QUERIES = 896
WINDOW = 640
HALF_COLS = 576
AUG = 80
PADDED = 512
LOOK = 2
QSCALE = math.log2(math.e) / math.sqrt(HEAD_DIM)
NT = (((1,), (1,)), ((), ()))
TN = (((0,), (0,)), ((), ()))
BF16 = jnp.bfloat16
F32 = jnp.float32
VMEM = pl.BlockSpec(memory_space=pltpu.VMEM)
SMEM = pl.BlockSpec(memory_space=pltpu.SMEM)
HBM = pl.BlockSpec(memory_space=pltpu.HBM)
EXCESS = 64.0


def params(mebibytes):
    return pltpu.CompilerParams(vmem_limit_bytes=mebibytes * 1024 * 1024)


def modulate(values, shift_vec, scale_vec):
    values = values.astype(F32)
    average = jnp.mean(values, axis=-1, keepdims=True)
    centred = values - average
    variance = jnp.mean(centred * centred, axis=-1, keepdims=True)
    normed = centred * lax.rsqrt(variance + 1e-06)
    return (normed * (1.0 + scale_vec) + shift_vec).astype(BF16)


def window_copy(w_hbm, third, core, place, sem):
    start = pl.multiple_of(third * WIDTH + core * 512, 128)
    return pltpu.make_async_copy(w_hbm.at[:, pl.ds(start, WINDOW)], place, sem)


def twice(x):
    return x.astype(BF16), jnp.concatenate([x[:, WINDOW - 64 :], x[:, : WINDOW - 64]], axis=1).astype(BF16)


def head_operands(head, core, q_ref, blocks):
    offset = head * HEAD_DIM + core * 64
    turned = (head + core) % 2
    inside = offset + 64 * turned
    start = pl.multiple_of(inside // 128 * 128, 128)
    inside = inside - start
    lane = lax.broadcasted_iota(jnp.int32, (1, 128), 1)
    mine = (lane >= inside) & (lane < inside + HEAD_DIM)
    queries = jnp.where(mine, q_ref[turned, :, pl.ds(start, 128)], jnp.zeros((), BF16))
    keys, values = [], []
    for k_ref, vt_ref in blocks:
        keys.append(k_ref[turned, :, pl.ds(start, 128)])
        first = lax.broadcasted_iota(jnp.int32, (AUG - HEAD_DIM, vt_ref.shape[1]), 0) == 0
        vt = vt_ref[pl.ds(pl.multiple_of(offset, 8), HEAD_DIM), :]
        values.append(jnp.concatenate([vt, jnp.where(first, 1.0, 0.0)], axis=0).astype(BF16))
    return queries, keys, values


def attend_heads(heads, halves, core, q_ref, blocks, old, known_top):
    operands = [head_operands(head, core, q_ref, blocks) for head in heads]
    items = [(i, half) for i in range(len(heads)) for half in halves]

    def score(item):
        i, half = item
        queries, keys, _ = operands[i]
        part = queries[half * ROWS : (half + 1) * ROWS]
        return [lax.dot_general(k, part, NT, preferred_element_type=F32) for k in keys]

    out = []
    ahead = [score(item) for item in items[:LOOK]]
    for n, (i, half) in enumerate(items):
        scores = ahead.pop(0)
        if n + LOOK < len(items):
            ahead.append(score(items[n + LOOK]))
        tops = [jnp.max(part, axis=0, keepdims=True) for part in scores]
        top = tops[0]
        for more in tops[1:]:
            top = jnp.maximum(top, more)
        total = None
        reference = top
        if old is not None:
            acc_ref, top_ref = old
            before = top_ref[half, heads[i], 0:1, :]
            total = acc_ref[half, heads[i]]
            if known_top:
                reference = before
            else:
                reference = jnp.maximum(top, before)
                total = total * jnp.exp2(before - reference)
        for value, part in zip(operands[i][2], scores):
            term = jnp.dot(value, jnp.exp2(part - reference).astype(BF16), preferred_element_type=F32)
            total = term if total is None else total + term
        out.append((total, reference, top))
    return out


def keys_values(xn, w_ref, k_ref, vt_ref):
    packed = jnp.dot(xn, w_ref[...], preferred_element_type=F32)
    k_ref[0], k_ref[1] = twice(packed[:, :WINDOW])
    vt_ref[...] = packed[:, WINDOW:].T


def near_kernel(
    core_ref, xo_hbm, xp_ref, mod_hbm, w_hbm, next_hbm, q_ref, acc_ref, top_ref, mod_ref, w_ref, next_ref, wq_ref, xo_ref, xn_ref, k_ref, vt_ref, sems
):
    core = core_ref[0]
    own = pltpu.make_async_copy(xo_hbm, xo_ref, sems.at[3])
    mod = pltpu.make_async_copy(mod_hbm, mod_ref, sems.at[4])
    mod.start()
    own.start()
    copies = [
        window_copy(w_hbm, 0, core, wq_ref, sems.at[0]),
        window_copy(w_hbm, 1, core, w_ref.at[:, :WINDOW], sems.at[1]),
        window_copy(w_hbm, 2, core, w_ref.at[:, WINDOW:], sems.at[2]),
    ]
    for copy in copies:
        copy.start()
    following = pltpu.make_async_copy(next_hbm, next_ref, sems.at[5])
    following.start()
    mod.wait()
    xn_ref[ROWS:, :] = modulate(xp_ref[...], mod_ref[0:1, :], mod_ref[1:2, :])
    own.wait()
    xn_ref[0:ROWS, :] = modulate(xo_ref[...], mod_ref[0:1, :], mod_ref[1:2, :])
    copies[0].wait()
    queries = jnp.dot(xn_ref[...], wq_ref[...], preferred_element_type=F32)
    q_ref[0], q_ref[1] = twice(queries * QSCALE)
    copies[1].wait()
    copies[2].wait()
    keys_values(xn_ref[...], w_ref, k_ref, vt_ref)


    def some(p, carry):
        heads = [2 * p + i for i in range(2)]
        results = attend_heads(heads, (0, 1), core, q_ref, ((k_ref, vt_ref),), None, False)
        for n, (total, top, _) in enumerate(results):
            acc_ref[n % 2, heads[n // 2]] = total
            top_ref[n % 2, heads[n // 2]] = jnp.broadcast_to(top, (8, ROWS))
        return carry

    lax.fori_loop(0, 8 // 2, some, 0)
    following.wait()


def near(core, xo, xp, mod, w, following):
    return pl.pallas_call(
        near_kernel,
        in_specs=[SMEM, HBM, VMEM, HBM, HBM, HBM],
        out_specs=[VMEM] * 6,
        out_shape=[
            jax.ShapeDtypeStruct((2, QUERIES, WINDOW), BF16),
            jax.ShapeDtypeStruct((2, 8, AUG, ROWS), F32),
            jax.ShapeDtypeStruct((2, 8, 8, ROWS), F32),
            jax.ShapeDtypeStruct((6, WIDTH), F32),
            jax.ShapeDtypeStruct((WIDTH, 2 * WINDOW), BF16),
            jax.ShapeDtypeStruct((WIDTH, 3 * WIDTH), BF16),
        ],
        scratch_shapes=[
            pltpu.VMEM((WIDTH, WINDOW), BF16),
            pltpu.VMEM((ROWS, WIDTH), BF16),
            pltpu.VMEM((QUERIES, WIDTH), BF16),
            pltpu.VMEM((2, QUERIES, WINDOW), BF16),
            pltpu.VMEM((WINDOW, QUERIES), F32),
            pltpu.SemaphoreType.DMA((6,)),
        ],
        compiler_params=params(36),
        cost_estimate=pl.CostEstimate(flops=1_000_000, bytes_accessed=100_000, transcendentals=0),
        name="near_tokens",
    )(core, xo, xp, mod, w, following)


def project_kernel(x_ref, mod_ref, w_ref, k_ref, vt_ref):
    xn = modulate(x_ref[...], mod_ref[0:1, :], mod_ref[1:2, :])
    keys_values(xn, w_ref, k_ref, vt_ref)


def project(x, mod, w):
    return pl.pallas_call(
        project_kernel,
        in_specs=[VMEM] * 3,
        out_specs=[VMEM] * 2,
        out_shape=[jax.ShapeDtypeStruct((2, ROWS, WINDOW), BF16), jax.ShapeDtypeStruct((WINDOW, ROWS), F32)],
        compiler_params=params(14),
        cost_estimate=pl.CostEstimate(flops=1_000_000, bytes_accessed=100_000, transcendentals=0),
        name="far_keys",
    )(x, mod, w)


def attend_far(half, core, q_ref, blocks, acc_ref, top_ref, out_ref, over_ref):
    def attend(first, count, known_top):
        heads = [first + i for i in range(count)]
        done = []
        for total, reference, top in attend_heads(heads, (half,), core, q_ref, blocks, (acc_ref, top_ref), known_top):
            if known_top:
                over_ref[0:1, :] = jnp.maximum(over_ref[0:1, :], top - reference)
            done.append(total[:HEAD_DIM] / total[HEAD_DIM : HEAD_DIM + 1])
        for i in range(0, count, 2):
            rows = pl.ds(pl.multiple_of((first + i) * HEAD_DIM, 16), 2 * HEAD_DIM)
            out_ref[rows, :ROWS] = jnp.concatenate(done[i : i + 2], axis=0).astype(BF16)

    over_ref[...] = jnp.zeros_like(over_ref)
    attend(0, 8, True)

    @pl.when(jnp.max(over_ref[...]) > EXCESS)
    def _():
        def pair(p, carry):
            attend(2 * p, 2, False)
            return carry

        lax.fori_loop(0, 4, pair, 0)


def far_peer_kernel(
    core_ref, x_ref, mod_ref, w_ref, k1_ref, vt1_ref, q_ref, acc_ref, top_ref, out_ref, k_ref, vt_ref, over_ref
):
    xn = modulate(x_ref[...], mod_ref[0:1, :], mod_ref[1:2, :])
    keys_values(xn, w_ref, k_ref, vt_ref)
    out_ref[:, ROWS:] = jnp.zeros((HALF_COLS, PADDED - ROWS), BF16)
    blocks = ((k1_ref, vt1_ref), (k_ref, vt_ref))
    attend_far(1, core_ref[0], q_ref, blocks, acc_ref, top_ref, out_ref, over_ref)


def far_peer(core, x, mod, w, k1, vt1, q, acc, top):
    return pl.pallas_call(
        far_peer_kernel,
        in_specs=[SMEM] + [VMEM] * 8,
        out_specs=[VMEM] * 3,
        out_shape=[
            jax.ShapeDtypeStruct((HALF_COLS, PADDED), BF16),
            jax.ShapeDtypeStruct((2, ROWS, WINDOW), BF16),
            jax.ShapeDtypeStruct((WINDOW, ROWS), F32),
        ],
        scratch_shapes=[pltpu.VMEM((8, ROWS), F32)],
        compiler_params=params(28),
        cost_estimate=pl.CostEstimate(flops=10_000_000_000, bytes_accessed=10_000_000, transcendentals=3_200_000),
        name="far_peer_queries",
    )(core, x, mod, w, k1, vt1, q, acc, top)


def far_own_kernel(core_ref, k1_ref, vt1_ref, k2_ref, vt2_ref, q_ref, acc_ref, top_ref, out_ref, over_ref):
    blocks = ((k1_ref, vt1_ref), (k2_ref, vt2_ref))
    attend_far(0, core_ref[0], q_ref, blocks, acc_ref, top_ref, out_ref, over_ref)


def far_own(core, k1, vt1, k2, vt2, q, acc, top):
    return pl.pallas_call(
        far_own_kernel,
        in_specs=[SMEM] + [VMEM] * 7,
        out_specs=VMEM,
        out_shape=jax.ShapeDtypeStruct((HALF_COLS, ROWS), BF16),
        scratch_shapes=[pltpu.VMEM((8, ROWS), F32)],
        compiler_params=params(24),
        cost_estimate=pl.CostEstimate(flops=8_000_000_000, bytes_accessed=5_000_000, transcendentals=3_200_000),
        name="far_own_queries",
    )(core, k1, vt1, k2, vt2, q, acc, top)


def join_kernel(core_ref, mine_ref, other_ref, x_ref, mod_ref, wo_ref, out_ref, kept_ref, att_ref):
    core = core_ref[0]
    att_ref[pl.ds(pl.multiple_of(core * HALF_COLS, 16), HALF_COLS), :] = mine_ref[...]
    att_ref[pl.ds(pl.multiple_of((1 - core) * HALF_COLS, 16), HALF_COLS), :] = other_ref[:, :ROWS]
    projected = lax.dot_general(att_ref[...], wo_ref[...], TN, preferred_element_type=F32)
    middle = x_ref[...].astype(F32) + mod_ref[2:3, :] * projected
    kept_ref[...] = middle.astype(BF16)
    for d in range(16):
        for i in range(7):
            out_ref[d, i] = middle[28 * d + 4 * i : 28 * d + 4 * i + 4].astype(BF16)


def join(core, mine, other, x, mod, wo):
    return pl.pallas_call(
        join_kernel,
        in_specs=[SMEM] + [VMEM] * 5,
        out_specs=[VMEM] * 2,
        out_shape=[jax.ShapeDtypeStruct((16, 7, 4, WIDTH), BF16), jax.ShapeDtypeStruct((ROWS, WIDTH), BF16)],
        scratch_shapes=[pltpu.VMEM((WIDTH, ROWS), BF16)],
        compiler_params=params(14),
        cost_estimate=pl.CostEstimate(flops=1_200_000_000, bytes_accessed=6_000_000, transcendentals=0),
        name="spatial_out",
    )(core, mine, other, x, mod, wo)


def temporal_kernel(mid_ref, mod_ref, w_ref, out_ref, x_ref, q_ref, k_ref, vt_ref, att_ref):
    for f in range(16):
        for i in range(7):
            at = ((i // 2 * 16) + f) * 8 + i % 2 * 4 if i < 6 else 384 + 4 * f
            x_ref[at : at + 4, :] = mid_ref[f, i].astype(F32)
    xn = modulate(x_ref[...], mod_ref[3:4, :], mod_ref[4:5, :])
    packed = jnp.dot(xn, w_ref[...], preferred_element_type=F32)
    q_ref[:, ROWS:] = jnp.zeros((WIDTH, PADDED - ROWS), BF16)
    q_ref[:, :ROWS] = (packed[:, :WIDTH] * QSCALE).T.astype(BF16)
    k_ref[...] = packed[:, WIDTH : 2 * WIDTH].astype(BF16)
    vt_ref[...] = packed[:, 2 * WIDTH :].T

    row = lax.broadcasted_iota(jnp.int32, (256, 1), 0)
    none = jnp.zeros((), BF16)

    def rows_of(g):
        return slice(g * 128, min(g * 128 + 128, ROWS))

    def score(g, p):
        queries = q_ref[128 * p : 128 * p + 256, g * 128 : g * 128 + 128]
        inside = 16 * p
        first = jnp.where((row >= inside) & (row < inside + HEAD_DIM), queries, none)
        second = jnp.where((row >= inside + HEAD_DIM) & (row < inside + 2 * HEAD_DIM), queries, none)
        keys = k_ref[rows_of(g), 128 * p : 128 * p + 256]
        return jnp.dot(keys, jnp.concatenate([first, second], axis=1), preferred_element_type=F32)

    def weigh(g, scores):
        every = 8 if g < 3 else 4
        shape = scores.shape
        key_token = lax.broadcasted_iota(jnp.int32, shape, 0) % every
        same = key_token == lax.broadcasted_iota(jnp.int32, shape, 1) % every
        scores = jnp.where(same, scores, -1e30)
        top = jnp.max(scores, axis=0, keepdims=True)
        return jnp.exp2(scores - top).astype(BF16)

    def value(g, p, weights):
        at = 2 * HEAD_DIM * p
        tail = jnp.where(lax.broadcasted_iota(jnp.int32, (AUG - HEAD_DIM, weights.shape[0]), 0) == 0, 1.0, 0.0)
        first = vt_ref[at : at + HEAD_DIM, rows_of(g)]
        second = vt_ref[at + HEAD_DIM : at + 2 * HEAD_DIM, rows_of(g)]
        values = jnp.concatenate([first, tail, second, tail], axis=0).astype(BF16)
        return jnp.dot(values, weights, preferred_element_type=F32)

    def finish(g, p, total):
        at = 2 * HEAD_DIM * p
        first = total[:HEAD_DIM, :128] / total[HEAD_DIM : HEAD_DIM + 1, :128]
        second = total[AUG : AUG + HEAD_DIM, 128:] / total[AUG + HEAD_DIM : AUG + HEAD_DIM + 1, 128:]
        att_ref[at : at + HEAD_DIM, g * 128 : g * 128 + 128] = first
        att_ref[at + HEAD_DIM : at + 2 * HEAD_DIM, g * 128 : g * 128 + 128] = second

    def send(g):
        rows = att_ref[:, g * 128 : g * 128 + 128].T
        for f in range(16):
            if g == 3:
                out_ref[f, 6] = rows[4 * f : 4 * f + 4].astype(BF16)
            else:
                out_ref[f, 2 * g] = rows[8 * f : 8 * f + 4].astype(BF16)
                out_ref[f, 2 * g + 1] = rows[8 * f + 4 : 8 * f + 8].astype(BF16)

    order = [(g, p) for g in range(4) for p in range(8)]
    apart = 4
    scores, totals = {}, {}
    for i in range(len(order) + 2 * apart):
        if i < len(order):
            scores[i] = score(*order[i])
        j = i - apart
        if 0 <= j < len(order):
            g, p = order[j]
            totals[j] = value(g, p, weigh(g, scores.pop(j)))
        k = i - 2 * apart
        if 0 <= k < len(order):
            finish(*order[k], totals.pop(k))
            if order[k][1] == 7:
                send(order[k][0])


def temporal(mid, mod, w):
    return pl.pallas_call(
        temporal_kernel,
        in_specs=[VMEM] * 3,
        out_specs=VMEM,
        out_shape=jax.ShapeDtypeStruct((16, 7, 4, WIDTH), BF16),
        scratch_shapes=[
            pltpu.VMEM((ROWS, WIDTH), F32),
            pltpu.VMEM((WIDTH, PADDED), BF16),
            pltpu.VMEM((ROWS, WIDTH), BF16),
            pltpu.VMEM((WIDTH, ROWS), F32),
            pltpu.VMEM((WIDTH, PADDED), F32),
        ],
        compiler_params=params(26),
        cost_estimate=pl.CostEstimate(flops=5_000_000_000, bytes_accessed=10_000_000, transcendentals=1_000_000),
        name="temporal_attention",
    )(mid, mod, w)


def last_kernel(att_ref, mid_ref, mod_ref, wo_ref, out_ref, rows_ref):
    for part in range(2):
        rows = slice(part * ROWS // 2, (part + 1) * ROWS // 2)
        for d in range(8 * part, 8 * part + 8):
            for i in range(7):
                rows_ref[28 * d + 4 * i : 28 * d + 4 * i + 4, :] = att_ref[d, i].astype(F32)
        projected = jnp.dot(rows_ref[rows, :].astype(BF16), wo_ref[...], preferred_element_type=F32)
        out_ref[rows, :] = (mid_ref[rows, :].astype(F32) + mod_ref[5:6, :] * projected).astype(BF16)


def last(att, mid, mod, wo):
    return pl.pallas_call(
        last_kernel,
        in_specs=[VMEM] * 4,
        out_specs=VMEM,
        out_shape=jax.ShapeDtypeStruct((ROWS, WIDTH), BF16),
        scratch_shapes=[pltpu.VMEM((ROWS, WIDTH), F32)],
        compiler_params=params(14),
        cost_estimate=pl.CostEstimate(flops=1_200_000_000, bytes_accessed=6_000_000, transcendentals=0),
        name="temporal_out",
    )(att, mid, mod, wo)


def local(clip, modulation, w_qkv_s, w_out_s, w_qkv_t, w_out_t):
    own = clip[0]
    core = (lax.axis_index("head") % 2).astype(jnp.int32).reshape(1)
    swap_chip = [(0, 2), (1, 3), (2, 0), (3, 1)]
    swap_core = [(0, 1), (1, 0), (2, 3), (3, 2)]
    peer = lax.ppermute(own, "head", swap_core)
    there = lax.ppermute(own, "head", swap_chip)
    q, acc, top, mod, w, w_t = near(core, own, peer, modulation, w_qkv_s, w_qkv_t)
    there, q = lax.optimization_barrier((there, q))
    k1, vt1 = project(there, mod, w)
    there_peer = lax.ppermute(there, "head", swap_core)
    theirs, k2, vt2 = far_peer(core, there_peer, mod, w, k1, vt1, q, acc, top)
    other = lax.ppermute(theirs, "head", swap_core)
    mine = far_own(core, k1, vt1, k2, vt2, q, acc, top)
    middle, kept = join(core, mine, other, own, mod, w_out_s)
    block = lax.all_to_all(middle, "tm", split_axis=0, concat_axis=0, tiled=True)
    attended = temporal(block, mod, w_t)
    back = lax.all_to_all(attended, "tm", split_axis=0, concat_axis=0, tiled=True)
    return last(back, kept, mod, w_out_t).reshape(1, ROWS, WIDTH)


def solution(mesh):
    placed = (P(("dp", "tm"), "head", None), P("dp", None), P(), P(), P(), P())
    return jax.shard_map(
        local, mesh=mesh, in_specs=placed, out_specs=P(("dp", "tm"), "head", None), check_vma=False
    )
```

```python
import math

import jax
import jax.numpy as jnp
from jax import lax
from jax.experimental import pallas as pl
from jax.experimental.pallas import tpu as pltpu
from jax.sharding import PartitionSpec as P

HEADS = 16
HEAD_DIM = 72
WIDTH = 1152
ROWS = 448
QUERIES = 896
WINDOW = 640
HALF_COLS = 576
AUG = 80
PADDED = 512
LOOK = 4
QSCALE = math.log2(math.e) / math.sqrt(HEAD_DIM)
NT = (((1,), (1,)), ((), ()))
TN = (((0,), (0,)), ((), ()))
BF16 = jnp.bfloat16
F32 = jnp.float32
VMEM = pl.BlockSpec(memory_space=pltpu.VMEM)
SMEM = pl.BlockSpec(memory_space=pltpu.SMEM)
HBM = pl.BlockSpec(memory_space=pltpu.HBM)
EXCESS = 64.0


def params(mebibytes):
    return pltpu.CompilerParams(vmem_limit_bytes=mebibytes * 1024 * 1024)


def modulate(values, shift_vec, scale_vec):
    values = values.astype(F32)
    average = jnp.mean(values, axis=-1, keepdims=True)
    centred = values - average
    variance = jnp.mean(centred * centred, axis=-1, keepdims=True)
    normed = centred * lax.rsqrt(variance + 1e-06)
    return (normed * (1.0 + scale_vec) + shift_vec).astype(BF16)


def window_copy(w_hbm, third, core, place, sem):
    start = pl.multiple_of(third * WIDTH + core * 512, 128)
    return pltpu.make_async_copy(w_hbm.at[:, pl.ds(start, WINDOW)], place, sem)


def twice(x):
    return x.astype(BF16), jnp.concatenate([x[:, WINDOW - 64 :], x[:, : WINDOW - 64]], axis=1).astype(BF16)


def head_operands(head, core, q_ref, blocks):
    offset = head * HEAD_DIM + core * 64
    turned = (head + core) % 2
    inside = offset + 64 * turned
    start = pl.multiple_of(inside // 128 * 128, 128)
    inside = inside - start
    lane = lax.broadcasted_iota(jnp.int32, (1, 128), 1)
    mine = (lane >= inside) & (lane < inside + HEAD_DIM)
    queries = jnp.where(mine, q_ref[turned, :, pl.ds(start, 128)], jnp.zeros((), BF16))
    keys, values = [], []
    for k_ref, vt_ref in blocks:
        keys.append(k_ref[turned, :, pl.ds(start, 128)])
        first = lax.broadcasted_iota(jnp.int32, (AUG - HEAD_DIM, vt_ref.shape[1]), 0) == 0
        vt = vt_ref[pl.ds(pl.multiple_of(offset, 8), HEAD_DIM), :]
        values.append(jnp.concatenate([vt, jnp.where(first, 1.0, 0.0)], axis=0).astype(BF16))
    return queries, keys, values


def attend_heads(heads, halves, core, q_ref, blocks, old, known_top):
    operands = [head_operands(head, core, q_ref, blocks) for head in heads]
    items = [(i, half) for i in range(len(heads)) for half in halves]

    def score(item):
        i, half = item
        queries, keys, _ = operands[i]
        part = queries[half * ROWS : (half + 1) * ROWS]
        return [lax.dot_general(k, part, NT, preferred_element_type=F32) for k in keys]

    out = []
    ahead = [score(item) for item in items[:LOOK]]
    for n, (i, half) in enumerate(items):
        scores = ahead.pop(0)
        if n + LOOK < len(items):
            ahead.append(score(items[n + LOOK]))
        tops = [jnp.max(part, axis=0, keepdims=True) for part in scores]
        top = tops[0]
        for more in tops[1:]:
            top = jnp.maximum(top, more)
        total = None
        reference = top
        if old is not None:
            acc_ref, top_ref = old
            before = top_ref[half, heads[i], 0:1, :]
            total = acc_ref[half, heads[i]]
            if known_top:
                reference = before
            else:
                reference = jnp.maximum(top, before)
                total = total * jnp.exp2(before - reference)
        for value, part in zip(operands[i][2], scores):
            term = jnp.dot(value, jnp.exp2(part - reference).astype(BF16), preferred_element_type=F32)
            total = term if total is None else total + term
        out.append((total, reference, top))
    return out


def keys_values(xn, w_ref, k_ref, vt_ref):
    packed = jnp.dot(xn, w_ref[...], preferred_element_type=F32)
    k_ref[0], k_ref[1] = twice(packed[:, :WINDOW])
    vt_ref[...] = packed[:, WINDOW:].T


def near_kernel(
    core_ref, xo_hbm, xp_ref, mod_hbm, w_hbm, next_hbm, q_ref, acc_ref, top_ref, mod_ref, w_ref, next_ref, wq_ref, xo_ref, xn_ref, k_ref, vt_ref, sems
):
    core = core_ref[0]
    own = pltpu.make_async_copy(xo_hbm, xo_ref, sems.at[3])
    mod = pltpu.make_async_copy(mod_hbm, mod_ref, sems.at[4])
    mod.start()
    own.start()
    copies = [
        window_copy(w_hbm, 0, core, wq_ref, sems.at[0]),
        window_copy(w_hbm, 1, core, w_ref.at[:, :WINDOW], sems.at[1]),
        window_copy(w_hbm, 2, core, w_ref.at[:, WINDOW:], sems.at[2]),
    ]
    for copy in copies:
        copy.start()
    following = pltpu.make_async_copy(next_hbm, next_ref, sems.at[5])
    following.start()
    mod.wait()
    xn_ref[ROWS:, :] = modulate(xp_ref[...], mod_ref[0:1, :], mod_ref[1:2, :])
    own.wait()
    xn_ref[0:ROWS, :] = modulate(xo_ref[...], mod_ref[0:1, :], mod_ref[1:2, :])
    copies[0].wait()
    queries = jnp.dot(xn_ref[...], wq_ref[...], preferred_element_type=F32)
    q_ref[0], q_ref[1] = twice(queries * QSCALE)
    copies[1].wait()
    copies[2].wait()
    keys_values(xn_ref[...], w_ref, k_ref, vt_ref)


    def some(p, carry):
        heads = [2 * p + i for i in range(2)]
        results = attend_heads(heads, (0, 1), core, q_ref, ((k_ref, vt_ref),), None, False)
        for n, (total, top, _) in enumerate(results):
            acc_ref[n % 2, heads[n // 2]] = total
            top_ref[n % 2, heads[n // 2]] = jnp.broadcast_to(top, (8, ROWS))
        return carry

    lax.fori_loop(0, 8 // 2, some, 0)
    following.wait()


def near(core, xo, xp, mod, w, following):
    return pl.pallas_call(
        near_kernel,
        in_specs=[SMEM, HBM, VMEM, HBM, HBM, HBM],
        out_specs=[VMEM] * 6,
        out_shape=[
            jax.ShapeDtypeStruct((2, QUERIES, WINDOW), BF16),
            jax.ShapeDtypeStruct((2, 8, AUG, ROWS), F32),
            jax.ShapeDtypeStruct((2, 8, 8, ROWS), F32),
            jax.ShapeDtypeStruct((6, WIDTH), F32),
            jax.ShapeDtypeStruct((WIDTH, 2 * WINDOW), BF16),
            jax.ShapeDtypeStruct((WIDTH, 3 * WIDTH), BF16),
        ],
        scratch_shapes=[
            pltpu.VMEM((WIDTH, WINDOW), BF16),
            pltpu.VMEM((ROWS, WIDTH), BF16),
            pltpu.VMEM((QUERIES, WIDTH), BF16),
            pltpu.VMEM((2, QUERIES, WINDOW), BF16),
            pltpu.VMEM((WINDOW, QUERIES), F32),
            pltpu.SemaphoreType.DMA((6,)),
        ],
        compiler_params=params(36),
        cost_estimate=pl.CostEstimate(flops=1_000_000, bytes_accessed=100_000, transcendentals=0),
        name="near_tokens",
    )(core, xo, xp, mod, w, following)


def project_kernel(x_ref, mod_ref, w_ref, k_ref, vt_ref):
    xn = modulate(x_ref[...], mod_ref[0:1, :], mod_ref[1:2, :])
    keys_values(xn, w_ref, k_ref, vt_ref)


def project(x, mod, w):
    return pl.pallas_call(
        project_kernel,
        in_specs=[VMEM] * 3,
        out_specs=[VMEM] * 2,
        out_shape=[jax.ShapeDtypeStruct((2, ROWS, WINDOW), BF16), jax.ShapeDtypeStruct((WINDOW, ROWS), F32)],
        compiler_params=params(14),
        cost_estimate=pl.CostEstimate(flops=1_000_000, bytes_accessed=100_000, transcendentals=0),
        name="far_keys",
    )(x, mod, w)


def attend_far(half, core, q_ref, blocks, acc_ref, top_ref, out_ref, over_ref):
    def attend(first, count, known_top):
        heads = [first + i for i in range(count)]
        done = []
        for total, reference, top in attend_heads(heads, (half,), core, q_ref, blocks, (acc_ref, top_ref), known_top):
            if known_top:
                over_ref[0:1, :] = jnp.maximum(over_ref[0:1, :], top - reference)
            done.append(total[:HEAD_DIM] / total[HEAD_DIM : HEAD_DIM + 1])
        for i in range(0, count, 2):
            rows = pl.ds(pl.multiple_of((first + i) * HEAD_DIM, 16), 2 * HEAD_DIM)
            out_ref[rows, :ROWS] = jnp.concatenate(done[i : i + 2], axis=0).astype(BF16)

    over_ref[...] = jnp.zeros_like(over_ref)
    attend(0, 8, True)

    @pl.when(jnp.max(over_ref[...]) > EXCESS)
    def _():
        def pair(p, carry):
            attend(2 * p, 2, False)
            return carry

        lax.fori_loop(0, 4, pair, 0)


def far_peer_kernel(
    core_ref, x_ref, mod_ref, w_ref, k1_ref, vt1_ref, q_ref, acc_ref, top_ref, out_ref, k_ref, vt_ref, over_ref
):
    xn = modulate(x_ref[...], mod_ref[0:1, :], mod_ref[1:2, :])
    keys_values(xn, w_ref, k_ref, vt_ref)
    out_ref[:, ROWS:] = jnp.zeros((HALF_COLS, PADDED - ROWS), BF16)
    blocks = ((k1_ref, vt1_ref), (k_ref, vt_ref))
    attend_far(1, core_ref[0], q_ref, blocks, acc_ref, top_ref, out_ref, over_ref)


def far_peer(core, x, mod, w, k1, vt1, q, acc, top):
    return pl.pallas_call(
        far_peer_kernel,
        in_specs=[SMEM] + [VMEM] * 8,
        out_specs=[VMEM] * 3,
        out_shape=[
            jax.ShapeDtypeStruct((HALF_COLS, PADDED), BF16),
            jax.ShapeDtypeStruct((2, ROWS, WINDOW), BF16),
            jax.ShapeDtypeStruct((WINDOW, ROWS), F32),
        ],
        scratch_shapes=[pltpu.VMEM((8, ROWS), F32)],
        compiler_params=params(28),
        cost_estimate=pl.CostEstimate(flops=10_000_000_000, bytes_accessed=10_000_000, transcendentals=3_200_000),
        name="far_peer_queries",
    )(core, x, mod, w, k1, vt1, q, acc, top)


def far_own_kernel(core_ref, k1_ref, vt1_ref, k2_ref, vt2_ref, q_ref, acc_ref, top_ref, out_ref, over_ref):
    blocks = ((k1_ref, vt1_ref), (k2_ref, vt2_ref))
    attend_far(0, core_ref[0], q_ref, blocks, acc_ref, top_ref, out_ref, over_ref)


def far_own(core, k1, vt1, k2, vt2, q, acc, top):
    return pl.pallas_call(
        far_own_kernel,
        in_specs=[SMEM] + [VMEM] * 7,
        out_specs=VMEM,
        out_shape=jax.ShapeDtypeStruct((HALF_COLS, ROWS), BF16),
        scratch_shapes=[pltpu.VMEM((8, ROWS), F32)],
        compiler_params=params(24),
        cost_estimate=pl.CostEstimate(flops=8_000_000_000, bytes_accessed=5_000_000, transcendentals=3_200_000),
        name="far_own_queries",
    )(core, k1, vt1, k2, vt2, q, acc, top)


def join_kernel(core_ref, mine_ref, other_ref, x_ref, mod_ref, wo_ref, out_ref, kept_ref, att_ref):
    core = core_ref[0]
    att_ref[pl.ds(pl.multiple_of(core * HALF_COLS, 16), HALF_COLS), :] = mine_ref[...]
    att_ref[pl.ds(pl.multiple_of((1 - core) * HALF_COLS, 16), HALF_COLS), :] = other_ref[:, :ROWS]
    projected = lax.dot_general(att_ref[...], wo_ref[...], TN, preferred_element_type=F32)
    middle = x_ref[...].astype(F32) + mod_ref[2:3, :] * projected
    kept_ref[...] = middle.astype(BF16)
    for d in range(16):
        for i in range(7):
            out_ref[d, i] = middle[28 * d + 4 * i : 28 * d + 4 * i + 4].astype(BF16)


def join(core, mine, other, x, mod, wo):
    return pl.pallas_call(
        join_kernel,
        in_specs=[SMEM] + [VMEM] * 5,
        out_specs=[VMEM] * 2,
        out_shape=[jax.ShapeDtypeStruct((16, 7, 4, WIDTH), BF16), jax.ShapeDtypeStruct((ROWS, WIDTH), BF16)],
        scratch_shapes=[pltpu.VMEM((WIDTH, ROWS), BF16)],
        compiler_params=params(14),
        cost_estimate=pl.CostEstimate(flops=1_200_000_000, bytes_accessed=6_000_000, transcendentals=0),
        name="spatial_out",
    )(core, mine, other, x, mod, wo)


def temporal_kernel(mid_ref, mod_ref, w_ref, out_ref, x_ref, q_ref, k_ref, vt_ref, att_ref):
    for f in range(16):
        for i in range(7):
            at = ((i // 2 * 16) + f) * 8 + i % 2 * 4 if i < 6 else 384 + 4 * f
            x_ref[at : at + 4, :] = mid_ref[f, i].astype(F32)
    xn = modulate(x_ref[...], mod_ref[3:4, :], mod_ref[4:5, :])
    packed = jnp.dot(xn, w_ref[...], preferred_element_type=F32)
    q_ref[:, ROWS:] = jnp.zeros((WIDTH, PADDED - ROWS), BF16)
    q_ref[:, :ROWS] = (packed[:, :WIDTH] * QSCALE).T.astype(BF16)
    k_ref[...] = packed[:, WIDTH : 2 * WIDTH].astype(BF16)
    vt_ref[...] = packed[:, 2 * WIDTH :].T

    row = lax.broadcasted_iota(jnp.int32, (256, 1), 0)
    none = jnp.zeros((), BF16)

    def rows_of(g):
        return slice(g * 128, min(g * 128 + 128, ROWS))

    def score(g, p):
        queries = q_ref[128 * p : 128 * p + 256, g * 128 : g * 128 + 128]
        inside = 16 * p
        first = jnp.where((row >= inside) & (row < inside + HEAD_DIM), queries, none)
        second = jnp.where((row >= inside + HEAD_DIM) & (row < inside + 2 * HEAD_DIM), queries, none)
        keys = k_ref[rows_of(g), 128 * p : 128 * p + 256]
        return jnp.dot(keys, jnp.concatenate([first, second], axis=1), preferred_element_type=F32)

    def weigh(g, scores):
        every = 8 if g < 3 else 4
        shape = scores.shape
        key_token = lax.broadcasted_iota(jnp.int32, shape, 0) % every
        same = key_token == lax.broadcasted_iota(jnp.int32, shape, 1) % every
        scores = jnp.where(same, scores, -1e30)
        top = jnp.max(scores, axis=0, keepdims=True)
        return jnp.exp2(scores - top).astype(BF16)

    def value(g, p, weights):
        at = 2 * HEAD_DIM * p
        tail = jnp.where(lax.broadcasted_iota(jnp.int32, (AUG - HEAD_DIM, weights.shape[0]), 0) == 0, 1.0, 0.0)
        first = vt_ref[at : at + HEAD_DIM, rows_of(g)]
        second = vt_ref[at + HEAD_DIM : at + 2 * HEAD_DIM, rows_of(g)]
        values = jnp.concatenate([first, tail, second, tail], axis=0).astype(BF16)
        return jnp.dot(values, weights, preferred_element_type=F32)

    def finish(g, p, total):
        at = 2 * HEAD_DIM * p
        first = total[:HEAD_DIM, :128] / total[HEAD_DIM : HEAD_DIM + 1, :128]
        second = total[AUG : AUG + HEAD_DIM, 128:] / total[AUG + HEAD_DIM : AUG + HEAD_DIM + 1, 128:]
        att_ref[at : at + HEAD_DIM, g * 128 : g * 128 + 128] = first
        att_ref[at + HEAD_DIM : at + 2 * HEAD_DIM, g * 128 : g * 128 + 128] = second

    def send(g):
        rows = att_ref[:, g * 128 : g * 128 + 128].T
        for f in range(16):
            if g == 3:
                out_ref[f, 6] = rows[4 * f : 4 * f + 4].astype(BF16)
            else:
                out_ref[f, 2 * g] = rows[8 * f : 8 * f + 4].astype(BF16)
                out_ref[f, 2 * g + 1] = rows[8 * f + 4 : 8 * f + 8].astype(BF16)

    order = [(g, p) for g in range(4) for p in range(8)]
    apart = 8
    scores, totals = {}, {}
    for i in range(len(order) + 2 * apart):
        if i < len(order):
            scores[i] = score(*order[i])
        j = i - apart
        if 0 <= j < len(order):
            g, p = order[j]
            totals[j] = value(g, p, weigh(g, scores.pop(j)))
        k = i - 2 * apart
        if 0 <= k < len(order):
            finish(*order[k], totals.pop(k))
            if order[k][1] == 7:
                send(order[k][0])


def temporal(mid, mod, w):
    return pl.pallas_call(
        temporal_kernel,
        in_specs=[VMEM] * 3,
        out_specs=VMEM,
        out_shape=jax.ShapeDtypeStruct((16, 7, 4, WIDTH), BF16),
        scratch_shapes=[
            pltpu.VMEM((ROWS, WIDTH), F32),
            pltpu.VMEM((WIDTH, PADDED), BF16),
            pltpu.VMEM((ROWS, WIDTH), BF16),
            pltpu.VMEM((WIDTH, ROWS), F32),
            pltpu.VMEM((WIDTH, PADDED), F32),
        ],
        compiler_params=params(26),
        cost_estimate=pl.CostEstimate(flops=5_000_000_000, bytes_accessed=10_000_000, transcendentals=1_000_000),
        name="temporal_attention",
    )(mid, mod, w)


def last_kernel(att_ref, mid_ref, mod_ref, wo_ref, out_ref, rows_ref):
    for part in range(2):
        rows = slice(part * ROWS // 2, (part + 1) * ROWS // 2)
        for d in range(8 * part, 8 * part + 8):
            for i in range(7):
                rows_ref[28 * d + 4 * i : 28 * d + 4 * i + 4, :] = att_ref[d, i].astype(F32)
        projected = jnp.dot(rows_ref[rows, :].astype(BF16), wo_ref[...], preferred_element_type=F32)
        out_ref[rows, :] = (mid_ref[rows, :].astype(F32) + mod_ref[5:6, :] * projected).astype(BF16)


def last(att, mid, mod, wo):
    return pl.pallas_call(
        last_kernel,
        in_specs=[VMEM] * 4,
        out_specs=VMEM,
        out_shape=jax.ShapeDtypeStruct((ROWS, WIDTH), BF16),
        scratch_shapes=[pltpu.VMEM((ROWS, WIDTH), F32)],
        compiler_params=params(14),
        cost_estimate=pl.CostEstimate(flops=1_200_000_000, bytes_accessed=6_000_000, transcendentals=0),
        name="temporal_out",
    )(att, mid, mod, wo)


def local(clip, modulation, w_qkv_s, w_out_s, w_qkv_t, w_out_t):
    own = clip[0]
    core = (lax.axis_index("head") % 2).astype(jnp.int32).reshape(1)
    swap_chip = [(0, 2), (1, 3), (2, 0), (3, 1)]
    swap_core = [(0, 1), (1, 0), (2, 3), (3, 2)]
    peer = lax.ppermute(own, "head", swap_core)
    there = lax.ppermute(own, "head", swap_chip)
    q, acc, top, mod, w, w_t = near(core, own, peer, modulation, w_qkv_s, w_qkv_t)
    there, q = lax.optimization_barrier((there, q))
    k1, vt1 = project(there, mod, w)
    there_peer = lax.ppermute(there, "head", swap_core)
    theirs, k2, vt2 = far_peer(core, there_peer, mod, w, k1, vt1, q, acc, top)
    other = lax.ppermute(theirs, "head", swap_core)
    mine = far_own(core, k1, vt1, k2, vt2, q, acc, top)
    middle, kept = join(core, mine, other, own, mod, w_out_s)
    block = lax.all_to_all(middle, "tm", split_axis=0, concat_axis=0, tiled=True)
    attended = temporal(block, mod, w_t)
    back = lax.all_to_all(attended, "tm", split_axis=0, concat_axis=0, tiled=True)
    return last(back, kept, mod, w_out_t).reshape(1, ROWS, WIDTH)


def solution(mesh):
    placed = (P(("dp", "tm"), "head", None), P("dp", None), P(), P(), P(), P())
    return jax.shard_map(
        local, mesh=mesh, in_specs=placed, out_specs=P(("dp", "tm"), "head", None), check_vma=False
    )
```

```python
import math

import jax
import jax.numpy as jnp
from jax import lax
from jax.experimental import pallas as pl
from jax.experimental.pallas import tpu as pltpu
from jax.sharding import PartitionSpec as P

HEADS = 16
HEAD_DIM = 72
WIDTH = 1152
ROWS = 448
QUERIES = 896
WINDOW = 640
HALF_COLS = 576
AUG = 80
PADDED = 512
LOOK = 2
QSCALE = math.log2(math.e) / math.sqrt(HEAD_DIM)
NT = (((1,), (1,)), ((), ()))
TN = (((0,), (0,)), ((), ()))
BF16 = jnp.bfloat16
F32 = jnp.float32
VMEM = pl.BlockSpec(memory_space=pltpu.VMEM)
SMEM = pl.BlockSpec(memory_space=pltpu.SMEM)
HBM = pl.BlockSpec(memory_space=pltpu.HBM)
EXCESS = 64.0


def params(mebibytes):
    return pltpu.CompilerParams(vmem_limit_bytes=mebibytes * 1024 * 1024)


def modulate(values, shift_vec, scale_vec):
    values = values.astype(F32)
    average = jnp.mean(values, axis=-1, keepdims=True)
    centred = values - average
    variance = jnp.mean(centred * centred, axis=-1, keepdims=True)
    normed = centred * lax.rsqrt(variance + 1e-06)
    return (normed * (1.0 + scale_vec) + shift_vec).astype(BF16)


def window_copy(w_hbm, third, core, place, sem):
    start = pl.multiple_of(third * WIDTH + core * 512, 128)
    return pltpu.make_async_copy(w_hbm.at[:, pl.ds(start, WINDOW)], place, sem)


def twice(x):
    return x.astype(BF16), jnp.concatenate([x[:, WINDOW - 64 :], x[:, : WINDOW - 64]], axis=1).astype(BF16)


def head_operands(head, core, q_ref, blocks):
    offset = head * HEAD_DIM + core * 64
    turned = (head + core) % 2
    inside = offset + 64 * turned
    start = pl.multiple_of(inside // 128 * 128, 128)
    inside = inside - start
    lane = lax.broadcasted_iota(jnp.int32, (1, 128), 1)
    mine = (lane >= inside) & (lane < inside + HEAD_DIM)
    queries = jnp.where(mine, q_ref[turned, :, pl.ds(start, 128)], jnp.zeros((), BF16))
    keys, values = [], []
    for k_ref, vt_ref in blocks:
        keys.append(k_ref[turned, :, pl.ds(start, 128)])
        first = lax.broadcasted_iota(jnp.int32, (AUG - HEAD_DIM, vt_ref.shape[1]), 0) == 0
        vt = vt_ref[pl.ds(pl.multiple_of(offset, 8), HEAD_DIM), :]
        values.append(jnp.concatenate([vt, jnp.where(first, 1.0, 0.0)], axis=0).astype(BF16))
    return queries, keys, values


def attend_heads(heads, halves, core, q_ref, blocks, old, known_top):
    operands = [head_operands(head, core, q_ref, blocks) for head in heads]
    items = [(i, half) for i in range(len(heads)) for half in halves]

    def score(item):
        i, half = item
        queries, keys, _ = operands[i]
        part = queries[half * ROWS : (half + 1) * ROWS]
        return [lax.dot_general(k, part, NT, preferred_element_type=F32) for k in keys]

    out = []
    ahead = [score(item) for item in items[:LOOK]]
    for n, (i, half) in enumerate(items):
        scores = ahead.pop(0)
        if n + LOOK < len(items):
            ahead.append(score(items[n + LOOK]))
        tops = [jnp.max(part, axis=0, keepdims=True) for part in scores]
        top = tops[0]
        for more in tops[1:]:
            top = jnp.maximum(top, more)
        total = None
        reference = top
        if old is not None:
            acc_ref, top_ref = old
            before = top_ref[half, heads[i], 0:1, :]
            total = acc_ref[half, heads[i]]
            if known_top:
                reference = before
            else:
                reference = jnp.maximum(top, before)
                total = total * jnp.exp2(before - reference)
        for value, part in zip(operands[i][2], scores):
            term = jnp.dot(value, jnp.exp2(part - reference).astype(BF16), preferred_element_type=F32)
            total = term if total is None else total + term
        out.append((total, reference, top))
    return out


def keys_values(xn, w_ref, k_ref, vt_ref):
    packed = jnp.dot(xn, w_ref[...], preferred_element_type=F32)
    k_ref[0], k_ref[1] = twice(packed[:, :WINDOW])
    vt_ref[...] = packed[:, WINDOW:].T


def near_kernel(
    core_ref, xo_hbm, xp_ref, mod_hbm, w_hbm, next_hbm, q_ref, acc_ref, top_ref, mod_ref, w_ref, next_ref, wq_ref, xo_ref, xn_ref, k_ref, vt_ref, sems
):
    core = core_ref[0]
    own = pltpu.make_async_copy(xo_hbm, xo_ref, sems.at[3])
    mod = pltpu.make_async_copy(mod_hbm, mod_ref, sems.at[4])
    mod.start()
    own.start()
    copies = [
        window_copy(w_hbm, 0, core, wq_ref, sems.at[0]),
        window_copy(w_hbm, 1, core, w_ref.at[:, :WINDOW], sems.at[1]),
        window_copy(w_hbm, 2, core, w_ref.at[:, WINDOW:], sems.at[2]),
    ]
    for copy in copies:
        copy.start()
    following = pltpu.make_async_copy(next_hbm, next_ref, sems.at[5])
    following.start()
    mod.wait()
    xn_ref[ROWS:, :] = modulate(xp_ref[...], mod_ref[0:1, :], mod_ref[1:2, :])
    own.wait()
    xn_ref[0:ROWS, :] = modulate(xo_ref[...], mod_ref[0:1, :], mod_ref[1:2, :])
    copies[0].wait()
    queries = jnp.dot(xn_ref[...], wq_ref[...], preferred_element_type=F32)
    q_ref[0], q_ref[1] = twice(queries * QSCALE)
    copies[1].wait()
    copies[2].wait()
    keys_values(xn_ref[...], w_ref, k_ref, vt_ref)


    def some(p, carry):
        heads = [2 * p + i for i in range(2)]
        results = attend_heads(heads, (0, 1), core, q_ref, ((k_ref, vt_ref),), None, False)
        for n, (total, top, _) in enumerate(results):
            acc_ref[n % 2, heads[n // 2]] = total
            top_ref[n % 2, heads[n // 2]] = jnp.broadcast_to(top, (8, ROWS))
        return carry

    lax.fori_loop(0, 8 // 2, some, 0)
    following.wait()


def near(core, xo, xp, mod, w, following):
    return pl.pallas_call(
        near_kernel,
        in_specs=[SMEM, HBM, VMEM, HBM, HBM, HBM],
        out_specs=[VMEM] * 6,
        out_shape=[
            jax.ShapeDtypeStruct((2, QUERIES, WINDOW), BF16),
            jax.ShapeDtypeStruct((2, 8, AUG, ROWS), F32),
            jax.ShapeDtypeStruct((2, 8, 8, ROWS), F32),
            jax.ShapeDtypeStruct((6, WIDTH), F32),
            jax.ShapeDtypeStruct((WIDTH, 2 * WINDOW), BF16),
            jax.ShapeDtypeStruct((WIDTH, 3 * WIDTH), BF16),
        ],
        scratch_shapes=[
            pltpu.VMEM((WIDTH, WINDOW), BF16),
            pltpu.VMEM((ROWS, WIDTH), BF16),
            pltpu.VMEM((QUERIES, WIDTH), BF16),
            pltpu.VMEM((2, QUERIES, WINDOW), BF16),
            pltpu.VMEM((WINDOW, QUERIES), F32),
            pltpu.SemaphoreType.DMA((6,)),
        ],
        compiler_params=params(36),
        cost_estimate=pl.CostEstimate(flops=1_000_000, bytes_accessed=100_000, transcendentals=0),
        name="near_tokens",
    )(core, xo, xp, mod, w, following)


def project_kernel(x_ref, mod_ref, w_ref, k_ref, vt_ref):
    xn = modulate(x_ref[...], mod_ref[0:1, :], mod_ref[1:2, :])
    keys_values(xn, w_ref, k_ref, vt_ref)


def project(x, mod, w):
    return pl.pallas_call(
        project_kernel,
        in_specs=[VMEM] * 3,
        out_specs=[VMEM] * 2,
        out_shape=[jax.ShapeDtypeStruct((2, ROWS, WINDOW), BF16), jax.ShapeDtypeStruct((WINDOW, ROWS), F32)],
        compiler_params=params(14),
        cost_estimate=pl.CostEstimate(flops=1_000_000, bytes_accessed=100_000, transcendentals=0),
        name="far_keys",
    )(x, mod, w)


def attend_far(half, core, q_ref, blocks, acc_ref, top_ref, out_ref, over_ref):
    def attend(first, count, known_top):
        heads = [first + i for i in range(count)]
        done = []
        for total, reference, top in attend_heads(heads, (half,), core, q_ref, blocks, (acc_ref, top_ref), known_top):
            if known_top:
                over_ref[0:1, :] = jnp.maximum(over_ref[0:1, :], top - reference)
            done.append(total[:HEAD_DIM] * (1.0 / total[HEAD_DIM : HEAD_DIM + 1]))
        for i in range(0, count, 2):
            rows = pl.ds(pl.multiple_of((first + i) * HEAD_DIM, 16), 2 * HEAD_DIM)
            out_ref[rows, :ROWS] = jnp.concatenate(done[i : i + 2], axis=0).astype(BF16)

    over_ref[...] = jnp.zeros_like(over_ref)
    attend(0, 8, True)

    @pl.when(jnp.max(over_ref[...]) > EXCESS)
    def _():
        def pair(p, carry):
            attend(2 * p, 2, False)
            return carry

        lax.fori_loop(0, 4, pair, 0)


def far_peer_kernel(
    core_ref, x_ref, mod_ref, w_ref, k1_ref, vt1_ref, q_ref, acc_ref, top_ref, out_ref, k_ref, vt_ref, over_ref
):
    xn = modulate(x_ref[...], mod_ref[0:1, :], mod_ref[1:2, :])
    keys_values(xn, w_ref, k_ref, vt_ref)
    out_ref[:, ROWS:] = jnp.zeros((HALF_COLS, PADDED - ROWS), BF16)
    blocks = ((k1_ref, vt1_ref), (k_ref, vt_ref))
    attend_far(1, core_ref[0], q_ref, blocks, acc_ref, top_ref, out_ref, over_ref)


def far_peer(core, x, mod, w, k1, vt1, q, acc, top):
    return pl.pallas_call(
        far_peer_kernel,
        in_specs=[SMEM] + [VMEM] * 8,
        out_specs=[VMEM] * 3,
        out_shape=[
            jax.ShapeDtypeStruct((HALF_COLS, PADDED), BF16),
            jax.ShapeDtypeStruct((2, ROWS, WINDOW), BF16),
            jax.ShapeDtypeStruct((WINDOW, ROWS), F32),
        ],
        scratch_shapes=[pltpu.VMEM((8, ROWS), F32)],
        compiler_params=params(28),
        cost_estimate=pl.CostEstimate(flops=10_000_000_000, bytes_accessed=10_000_000, transcendentals=3_200_000),
        name="far_peer_queries",
    )(core, x, mod, w, k1, vt1, q, acc, top)


def far_own_kernel(core_ref, k1_ref, vt1_ref, k2_ref, vt2_ref, q_ref, acc_ref, top_ref, out_ref, over_ref):
    blocks = ((k1_ref, vt1_ref), (k2_ref, vt2_ref))
    attend_far(0, core_ref[0], q_ref, blocks, acc_ref, top_ref, out_ref, over_ref)


def far_own(core, k1, vt1, k2, vt2, q, acc, top):
    return pl.pallas_call(
        far_own_kernel,
        in_specs=[SMEM] + [VMEM] * 7,
        out_specs=VMEM,
        out_shape=jax.ShapeDtypeStruct((HALF_COLS, ROWS), BF16),
        scratch_shapes=[pltpu.VMEM((8, ROWS), F32)],
        compiler_params=params(24),
        cost_estimate=pl.CostEstimate(flops=8_000_000_000, bytes_accessed=5_000_000, transcendentals=3_200_000),
        name="far_own_queries",
    )(core, k1, vt1, k2, vt2, q, acc, top)


def join_kernel(core_ref, mine_ref, other_ref, x_ref, mod_ref, wo_ref, out_ref, kept_ref, att_ref):
    core = core_ref[0]
    att_ref[pl.ds(pl.multiple_of(core * HALF_COLS, 16), HALF_COLS), :] = mine_ref[...]
    att_ref[pl.ds(pl.multiple_of((1 - core) * HALF_COLS, 16), HALF_COLS), :] = other_ref[:, :ROWS]
    projected = lax.dot_general(att_ref[...], wo_ref[...], TN, preferred_element_type=F32)
    middle = x_ref[...].astype(F32) + mod_ref[2:3, :] * projected
    kept_ref[...] = middle.astype(BF16)
    for d in range(16):
        for i in range(7):
            out_ref[d, i] = middle[28 * d + 4 * i : 28 * d + 4 * i + 4].astype(BF16)


def join(core, mine, other, x, mod, wo):
    return pl.pallas_call(
        join_kernel,
        in_specs=[SMEM] + [VMEM] * 5,
        out_specs=[VMEM] * 2,
        out_shape=[jax.ShapeDtypeStruct((16, 7, 4, WIDTH), BF16), jax.ShapeDtypeStruct((ROWS, WIDTH), BF16)],
        scratch_shapes=[pltpu.VMEM((WIDTH, ROWS), BF16)],
        compiler_params=params(14),
        cost_estimate=pl.CostEstimate(flops=1_200_000_000, bytes_accessed=6_000_000, transcendentals=0),
        name="spatial_out",
    )(core, mine, other, x, mod, wo)


def temporal_kernel(mid_ref, mod_ref, w_ref, out_ref, x_ref, q_ref, k_ref, vt_ref, att_ref):
    for f in range(16):
        for i in range(7):
            at = ((i // 2 * 16) + f) * 8 + i % 2 * 4 if i < 6 else 384 + 4 * f
            x_ref[at : at + 4, :] = mid_ref[f, i].astype(F32)
    xn = modulate(x_ref[...], mod_ref[3:4, :], mod_ref[4:5, :])
    packed = jnp.dot(xn, w_ref[...], preferred_element_type=F32)
    q_ref[:, ROWS:] = jnp.zeros((WIDTH, PADDED - ROWS), BF16)
    q_ref[:, :ROWS] = (packed[:, :WIDTH] * QSCALE).T.astype(BF16)
    k_ref[...] = packed[:, WIDTH : 2 * WIDTH].astype(BF16)
    vt_ref[...] = packed[:, 2 * WIDTH :].T

    row = lax.broadcasted_iota(jnp.int32, (256, 1), 0)
    none = jnp.zeros((), BF16)

    def rows_of(g):
        return slice(g * 128, min(g * 128 + 128, ROWS))

    def score(g, p):
        queries = q_ref[128 * p : 128 * p + 256, g * 128 : g * 128 + 128]
        inside = 16 * p
        first = jnp.where((row >= inside) & (row < inside + HEAD_DIM), queries, none)
        second = jnp.where((row >= inside + HEAD_DIM) & (row < inside + 2 * HEAD_DIM), queries, none)
        keys = k_ref[rows_of(g), 128 * p : 128 * p + 256]
        return jnp.dot(keys, jnp.concatenate([first, second], axis=1), preferred_element_type=F32)

    def weigh(g, scores):
        every = 8 if g < 3 else 4
        shape = scores.shape
        key_token = lax.broadcasted_iota(jnp.int32, shape, 0) % every
        same = key_token == lax.broadcasted_iota(jnp.int32, shape, 1) % every
        scores = jnp.where(same, scores, -1e30)
        top = jnp.max(scores, axis=0, keepdims=True)
        return jnp.exp2(scores - top).astype(BF16)

    def value(g, p, weights):
        at = 2 * HEAD_DIM * p
        tail = jnp.where(lax.broadcasted_iota(jnp.int32, (AUG - HEAD_DIM, weights.shape[0]), 0) == 0, 1.0, 0.0)
        first = vt_ref[at : at + HEAD_DIM, rows_of(g)]
        second = vt_ref[at + HEAD_DIM : at + 2 * HEAD_DIM, rows_of(g)]
        values = jnp.concatenate([first, tail, second, tail], axis=0).astype(BF16)
        return jnp.dot(values, weights, preferred_element_type=F32)

    def finish(g, p, total):
        at = 2 * HEAD_DIM * p
        first = total[:HEAD_DIM, :128] * (1.0 / total[HEAD_DIM : HEAD_DIM + 1, :128])
        second = total[AUG : AUG + HEAD_DIM, 128:] * (1.0 / total[AUG + HEAD_DIM : AUG + HEAD_DIM + 1, 128:])
        att_ref[at : at + HEAD_DIM, g * 128 : g * 128 + 128] = first
        att_ref[at + HEAD_DIM : at + 2 * HEAD_DIM, g * 128 : g * 128 + 128] = second

    def send(g):
        rows = att_ref[:, g * 128 : g * 128 + 128].T
        for f in range(16):
            if g == 3:
                out_ref[f, 6] = rows[4 * f : 4 * f + 4].astype(BF16)
            else:
                out_ref[f, 2 * g] = rows[8 * f : 8 * f + 4].astype(BF16)
                out_ref[f, 2 * g + 1] = rows[8 * f + 4 : 8 * f + 8].astype(BF16)

    order = [(g, p) for g in range(4) for p in range(8)]
    apart = 4
    scores, totals = {}, {}
    for i in range(len(order) + 2 * apart):
        if i < len(order):
            scores[i] = score(*order[i])
        j = i - apart
        if 0 <= j < len(order):
            g, p = order[j]
            totals[j] = value(g, p, weigh(g, scores.pop(j)))
        k = i - 2 * apart
        if 0 <= k < len(order):
            finish(*order[k], totals.pop(k))
            if order[k][1] == 7:
                send(order[k][0])


def temporal(mid, mod, w):
    return pl.pallas_call(
        temporal_kernel,
        in_specs=[VMEM] * 3,
        out_specs=VMEM,
        out_shape=jax.ShapeDtypeStruct((16, 7, 4, WIDTH), BF16),
        scratch_shapes=[
            pltpu.VMEM((ROWS, WIDTH), F32),
            pltpu.VMEM((WIDTH, PADDED), BF16),
            pltpu.VMEM((ROWS, WIDTH), BF16),
            pltpu.VMEM((WIDTH, ROWS), F32),
            pltpu.VMEM((WIDTH, PADDED), F32),
        ],
        compiler_params=params(26),
        cost_estimate=pl.CostEstimate(flops=5_000_000_000, bytes_accessed=10_000_000, transcendentals=1_000_000),
        name="temporal_attention",
    )(mid, mod, w)


def last_kernel(att_ref, mid_ref, mod_ref, wo_ref, out_ref, rows_ref):
    for part in range(2):
        rows = slice(part * ROWS // 2, (part + 1) * ROWS // 2)
        for d in range(8 * part, 8 * part + 8):
            for i in range(7):
                rows_ref[28 * d + 4 * i : 28 * d + 4 * i + 4, :] = att_ref[d, i].astype(F32)
        projected = jnp.dot(rows_ref[rows, :].astype(BF16), wo_ref[...], preferred_element_type=F32)
        out_ref[rows, :] = (mid_ref[rows, :].astype(F32) + mod_ref[5:6, :] * projected).astype(BF16)


def last(att, mid, mod, wo):
    return pl.pallas_call(
        last_kernel,
        in_specs=[VMEM] * 4,
        out_specs=VMEM,
        out_shape=jax.ShapeDtypeStruct((ROWS, WIDTH), BF16),
        scratch_shapes=[pltpu.VMEM((ROWS, WIDTH), F32)],
        compiler_params=params(14),
        cost_estimate=pl.CostEstimate(flops=1_200_000_000, bytes_accessed=6_000_000, transcendentals=0),
        name="temporal_out",
    )(att, mid, mod, wo)


def local(clip, modulation, w_qkv_s, w_out_s, w_qkv_t, w_out_t):
    own = clip[0]
    core = (lax.axis_index("head") % 2).astype(jnp.int32).reshape(1)
    swap_chip = [(0, 2), (1, 3), (2, 0), (3, 1)]
    swap_core = [(0, 1), (1, 0), (2, 3), (3, 2)]
    peer = lax.ppermute(own, "head", swap_core)
    there = lax.ppermute(own, "head", swap_chip)
    q, acc, top, mod, w, w_t = near(core, own, peer, modulation, w_qkv_s, w_qkv_t)
    there, q = lax.optimization_barrier((there, q))
    k1, vt1 = project(there, mod, w)
    there_peer = lax.ppermute(there, "head", swap_core)
    theirs, k2, vt2 = far_peer(core, there_peer, mod, w, k1, vt1, q, acc, top)
    other = lax.ppermute(theirs, "head", swap_core)
    mine = far_own(core, k1, vt1, k2, vt2, q, acc, top)
    middle, kept = join(core, mine, other, own, mod, w_out_s)
    block = lax.all_to_all(middle, "tm", split_axis=0, concat_axis=0, tiled=True)
    attended = temporal(block, mod, w_t)
    back = lax.all_to_all(attended, "tm", split_axis=0, concat_axis=0, tiled=True)
    return last(back, kept, mod, w_out_t).reshape(1, ROWS, WIDTH)


def solution(mesh):
    placed = (P(("dp", "tm"), "head", None), P("dp", None), P(), P(), P(), P())
    return jax.shard_map(
        local, mesh=mesh, in_specs=placed, out_specs=P(("dp", "tm"), "head", None), check_vma=False
    )
```
